256 devices in a mesh: dp: 64 (over x_lo, y, z), group: 4 (over x_hi, core).
Axes of the slice: x: 4 (x_hi: 2, x_lo: 2; x = x_hi * 2 + x_lo), y: 4, z: 8, core: 2. Of those that a mesh axis runs over, the one named last changes fastest.
Arguments:
- event: bfloat16 [12288, 1024], P('dp'), may hold values from -0.1875 to 0.1875
- lidar: bfloat16 [12288, 1024], P('dp'), may hold values from -0.1875 to 0.1875
- frame: bfloat16 [12288, 1024], P('dp'), may hold values from -0.1875 to 0.1875
- sample_ids: int32 [3, 12288], replicated, may hold values from 0 to 12287, each once within a row
- logit_scale: float32 [3], replicated, may hold values from 10 to 40
- logit_bias: float32 [3], replicated, may hold values from -4 to -1
Outputs:
- grad_event: float32 [12288, 1024], P('dp')
- grad_lidar: float32 [12288, 1024], P('dp')
- grad_frame: float32 [12288, 1024], P('dp')
The draws below stay inside these ranges and needn't reach their ends.
Inputs may be any that keep to these rules, and one draw needn't show every extreme that they name: Each row of sample_ids is a permutation of 0 to 12287, so every row has exactly one partner of its sample in each other modality.
All inputs are finite; a program needn't handle non-finite values.
Results may differ from the reference program's by a relative error of at most 0.0015.
Values may be sent and summed in bfloat16 or wider, within the bound.
A program may use at most 128 MiB of HBM per device.

```python
import math
import jax
import jax.numpy as jnp
from jax import lax

D = 1024
TOK_DEV = 192
TOKENS = 12288


def levels(key, extent, cuts, smallest, top_value):
    gain, own = 1.0, jax.random.fold_in(key, 6)
    for axis_at, parts in cuts:
        steps = jnp.exp(jax.random.uniform(jax.random.fold_in(own, axis_at), (parts,), jnp.float32, smallest / len(cuts), top_value / len(cuts)))
        gain = gain * jnp.repeat(steps, extent[axis_at] // parts).reshape([-1 if axis == axis_at else 1 for axis in range(len(extent))])
    return gain


def bell_draw(rng, extent, width, reach, shards=(), held_as=jnp.bfloat16):
    factor_of = levels(rng, extent, shards, -0.22, 0.18) if shards else 1.0
    drawn = jax.random.normal(rng, extent, jnp.float32) * width * factor_of
    return jnp.minimum(jnp.maximum(drawn, -reach), reach).astype(held_as)


def setup_inputs(seed: int = 0) -> dict:
    keys = jax.random.split(jax.random.key(seed), 7)
    event = bell_draw(keys[0], (TOKENS, D), D ** -0.5, 0.1875, ((0, 64),))
    lidar = bell_draw(keys[1], (TOKENS, D), D ** -0.5, 0.1875, ((0, 64),))
    frame = bell_draw(keys[2], (TOKENS, D), D ** -0.5, 0.1875, ((0, 64),))
    sample_ids = jax.vmap(lambda own: jax.random.permutation(own, TOKENS))(jax.random.split(keys[3], 3)).reshape((3, TOKENS)).astype(jnp.int32)
    logit_scale = jnp.clip(jnp.exp(jax.random.uniform(keys[4], (3,), jnp.float32, math.log(10.0), math.log(40.0))), 10.0, 40.0)
    logit_bias = jnp.clip(jax.random.uniform(keys[5], (3,), jnp.float32, -4.0, -1.0), -4.0, -1.0)
    return dict(event=event, lidar=lidar, frame=frame, sample_ids=sample_ids, logit_scale=logit_scale, logit_bias=logit_bias)


def pair_grad(own, own_ids, other, other_ids, scale, bias):
    blocks = own.reshape(TOKENS // TOK_DEV, TOK_DEV, own.shape[1])
    block_ids = own_ids.reshape(TOKENS // TOK_DEV, TOK_DEV)

    def one_block(inputs):
        rows, row_ids = inputs
        logits = jnp.einsum('id,jd->ij', rows, other, preferred_element_type=jnp.float32)
        shifted = scale * logits + bias
        labels = (row_ids[:, None] == other_ids[None, :]).astype(jnp.float32)
        coef = (jax.nn.sigmoid(shifted) - labels).astype(jnp.bfloat16)
        return scale * jnp.dot(coef, other, preferred_element_type=jnp.float32)
    return lax.map(one_block, (blocks, block_ids)).reshape(TOKENS, own.shape[1])

def reference(event, lidar, frame, sample_ids, logit_scale, logit_bias):
    modes = (event, lidar, frame)
    grads = []
    for first in range(3):
        total = jnp.zeros((TOKENS, event.shape[1]), jnp.float32)
        for second in range(3):
            if second != first:
                slot = first + second - 1
                total = total + pair_grad(modes[first], sample_ids[first], modes[second], sample_ids[second], logit_scale[slot], logit_bias[slot])
        grads.append(total)
    return (grads[0], grads[1], grads[2])
```

```python
import functools

import jax
import jax.numpy as jnp
from jax import lax
from jax.experimental import pallas as pl
from jax.experimental.pallas import tpu as pltpu
from jax.sharding import PartitionSpec as P

MESH = pl.DeviceIdType.MESH
ROWS = 192
HALF = 96
WIDTH = 1024
BLOCK = 768


class Place:
    def __init__(self):
        dp, group = lax.axis_index("dp"), lax.axis_index("group")
        self.xl, self.y, self.z = dp // 32, (dp // 8) % 4, dp % 8
        self.xh, self.c = group // 2, group % 2
        self.s = jnp.where(self.xl == 0, self.y, 7 - self.y)
        self.delta_c = (self.z + self.c + self.xh) % 2
        self.delta_a = (self.s + self.xh) % 2
        self.straight = self.c == self.xl

    def at(self, xh=None, xl=None, y=None, z=None, c=None):
        xh, xl = self.xh if xh is None else xh, self.xl if xl is None else xl
        y, z = self.y if y is None else y, self.z if z is None else z
        c = self.c if c is None else c
        return (xl * 32 + y * 8 + z, xh * 2 + c)

    def column(self, step):
        return self.at(z=(self.z + step + 8) % 8)

    def diagonal(self, step):
        s = (self.s + step + 8) % 8
        return self.at(
            xl=s // 4, y=jnp.where(s < 4, s, 7 - s), z=(self.z + step + 8) % 8
        )

    def across(self, step, y):
        x = (self.xh * 2 + self.xl + step + 4) % 4
        return self.at(xh=x // 2, xl=x % 2, y=y, c=1 - self.c)

    def other_core(self):
        return self.at(c=1 - self.c)

    def twin(self):
        return self.at(xh=1 - self.xh)


def remote(src, dst, send, recv, device):
    return pltpu.make_async_remote_copy(
        src_ref=src,
        dst_ref=dst,
        send_sem=send,
        recv_sem=recv,
        device_id=device,
        device_id_type=MESH,
    )


def signal(sem, device):
    pl.semaphore_signal(sem, inc=1, device_id=device, device_id_type=MESH)


def greet(at, twin, back):
    barrier = pltpu.get_barrier_semaphore()
    for step in (-1, 1):
        signal(barrier, at.column(step))
        signal(barrier, at.diagonal(step))
    signal(barrier, at.other_core())
    if twin:
        signal(barrier, at.twin())

    @pl.when(at.straight)
    def _():
        for step in range(1, 4):
            signal(barrier, at.at(y=(at.y + step) % 4))

    @pl.when(jnp.logical_not(at.straight))
    def _():
        for y in range(4):
            signal(barrier, at.across(1 if back else -1, y))

    pl.semaphore_wait(barrier, 5 + int(twin) + jnp.where(at.straight, 3, 4))


class RingGather:
    def __init__(self, place, delta, neighbour, far, own, slot, send, recv):
        self.place, self.delta, self.neighbour, self.far = place, delta, neighbour, far
        self.own, self.slot, self.send, self.recv = own, slot, send, recv

    def copy(self, direction, message, source, src=None):
        d = 0 if direction == self.far else 1
        dst = self.slot((source + 8) % 8)
        return remote(
            dst if src is None else src,
            dst,
            self.send.at[d, message],
            self.recv.at[d, message],
            self.neighbour(direction),
        )

    def start(self):
        @pl.when(self.delta == 0)
        def _():
            for direction in (self.far, -self.far):
                self.copy(direction, 0, self.place, self.own).start()

    def stage(self, st, arrived=None):
        message = (st - 1) // 2
        odd = st % 2

        @pl.when(self.delta == odd)
        def _():
            for direction in (self.far, -self.far):
                if direction != self.far and st > 3:
                    continue
                source = self.place - direction * st
                self.copy(direction, message, source).wait_recv()
                if st < (4 if direction == self.far else 3):
                    self.copy(direction, message + 1 - odd, source).start()
                if arrived is not None:
                    arrived((source + 8) % 8)

    def finish(self):
        for direction in (self.far, -self.far):
            for message in range(2):
                if direction != self.far and message == 1:

                    @pl.when(self.delta == 0)
                    def _():
                        self.copy(direction, 1, self.place).wait_send()

                else:
                    self.copy(direction, message, self.place).wait_send()


def gather_kernel(
    a_own, b_own, c_own, a_all, b_all, c_all,
    c_send, c_recv, a_send, a_recv, t_send, t_recv, b_send, b_recv, own_sem,
):
    at = Place()
    half = pl.ds(at.c * HALF, HALF)
    ring_c = RingGather(
        at.z, at.delta_c, at.column, 1, c_own, lambda q: c_all.at[q // 2], c_send, c_recv
    )
    ring_a = RingGather(
        at.s, at.delta_a, at.diagonal, -1, a_own.at[half], lambda q: a_all.at[q // 2, half], a_send, a_recv
    )
    own_c = pltpu.make_async_copy(c_own, c_all.at[at.z // 2], own_sem.at[0])
    own_a = pltpu.make_async_copy(a_own, a_all.at[at.s // 2], own_sem.at[1])
    own_b = pltpu.make_async_copy(b_own, b_all.at[at.y], own_sem.at[2])

    def pass_over(q):
        view = a_all.at[q // 2, half]
        return remote(view, view, t_send.at[q // 2], t_recv.at[q // 2], at.other_core())

    def taken_over(q):
        view = a_all.at[q // 2, pl.ds((1 - at.c) * HALF, HALF)]
        return remote(view, view, t_send.at[q // 2], t_recv.at[q // 2], at.other_core())

    def straight_copy(step):
        return remote(
            b_own, b_all.at[at.y], b_send.at[step], b_recv.at[at.y], at.at(y=(at.y + step) % 4)
        )

    def across_copy(y):
        return remote(
            b_own, b_all.at[at.y], b_send.at[y], b_recv.at[at.y], at.across(1, y)
        )

    def b_arrival(y):
        return remote(
            b_own, b_all.at[y], b_send.at[0], b_recv.at[y], at.other_core()
        )

    greet(at, twin=False, back=False)
    ring_c.start()
    ring_a.start()

    @pl.when(at.delta_c == 0)
    def _():
        own_c.start()

    @pl.when(at.delta_a == 0)
    def _():
        own_a.start()

    @pl.when(at.straight)
    def _():
        own_b.start()
        for step in range(1, 4):
            straight_copy(step).start()

    @pl.when(jnp.logical_not(at.straight))
    def _():
        for y in range(4):
            across_copy(y).start()

    for st in range(1, 5):
        ring_c.stage(st)
        ring_a.stage(st, lambda q: pass_over(q).start())
    ring_c.finish()
    ring_a.finish()

    @pl.when(at.delta_c == 0)
    def _():
        own_c.wait()

    @pl.when(at.delta_a == 0)
    def _():
        own_a.wait()

    @pl.when(at.straight)
    def _():
        own_b.wait()
        for step in range(1, 4):
            straight_copy(step).wait_send()
            b_arrival((at.y + step) % 4).wait_recv()

    @pl.when(jnp.logical_not(at.straight))
    def _():
        for y in range(4):
            across_copy(y).wait_send()
            b_arrival(y).wait_recv()

    for slot in range(4):

        @pl.when(jnp.logical_or(at.delta_a == 1, at.s // 2 != slot))
        def _():
            pass_over(2 * slot).wait_send()
            taken_over(2 * slot).wait_recv()


def gather(a, b, c):
    whole = jax.ShapeDtypeStruct((4, ROWS, WIDTH), jnp.bfloat16)
    hbm = pl.BlockSpec(memory_space=pl.ANY)
    dma = pltpu.SemaphoreType.DMA
    return pl.pallas_call(
        gather_kernel,
        out_shape=(whole, whole, whole),
        in_specs=[hbm] * 3,
        out_specs=(hbm, hbm, hbm),
        scratch_shapes=[
            dma((2, 2)), dma((2, 2)), dma((2, 2)), dma((2, 2)),
            dma((4,)), dma((4,)), dma((4,)), dma((4,)), dma((3,)),
        ],
        compiler_params=pltpu.CompilerParams(collective_id=0, has_side_effects=True),
    )(a, b, c)


TILE = 256


def compute_kernel(
    scale, bias, a_col, b_col, b_row, c_row, a, b, c, ga, gb, gc, coef
):
    def pair(left, right, left_ids, right_ids, p, g_left, g_right, new_left, new_right):
        def rows(i, _):
            span = pl.ds(pl.multiple_of(i * TILE, TILE), TILE)
            logits = lax.dot_general(
                left[span, :], right[...], (((1,), (1,)), ((), ())),
                preferred_element_type=jnp.float32,
            )
            u = scale[p] * logits + bias[p]
            label = (left_ids[span, :] == right_ids[...]).astype(jnp.float32)
            tile = (jax.nn.sigmoid(u) - label).astype(jnp.bfloat16)
            coef[span, :] = tile
            part = scale[p] * jnp.dot(
                tile, right[...], preferred_element_type=jnp.float32
            )
            g_left[span, :] = part if new_left else g_left[span, :] + part
            return 0

        lax.fori_loop(0, BLOCK // TILE, rows, 0)
        for i in range(BLOCK // TILE):
            span = pl.ds(i * TILE, TILE)
            part = scale[p] * lax.dot_general(
                coef[:, span], left[...], (((0,), (0,)), ((), ())),
                preferred_element_type=jnp.float32,
            )
            g_right[span, :] = part if new_right else g_right[span, :] + part

    pair(b, c, b_col, c_row, 2, gb, gc, True, True)
    pair(a, b, a_col, b_row, 0, ga, gb, True, False)
    pair(a, c, a_col, c_row, 1, ga, gc, False, False)


def compute(scale, bias, a_ids, b_ids, c_ids, a, b, c):
    vmem = pl.BlockSpec(memory_space=pltpu.VMEM)
    smem = pl.BlockSpec(memory_space=pltpu.SMEM)
    part = jax.ShapeDtypeStruct((BLOCK, WIDTH), jnp.float32)
    return pl.pallas_call(
        compute_kernel,
        out_shape=(part, part, part),
        in_specs=[smem, smem] + [vmem] * 7,
        out_specs=(vmem, vmem, vmem),
        scratch_shapes=[pltpu.VMEM((BLOCK, BLOCK), jnp.bfloat16)],
        compiler_params=pltpu.CompilerParams(vmem_limit_bytes=56 << 20),
    )(
        scale, bias, a_ids.reshape(BLOCK, 1), b_ids.reshape(BLOCK, 1),
        b_ids.reshape(1, BLOCK), c_ids.reshape(1, BLOCK), a, b, c,
    )


class RingReduce:
    def __init__(self, place, delta, neighbour, far, part, box, send, recv):
        self.place, self.delta, self.neighbour, self.far = place, delta, neighbour, far
        self.part, self.box, self.send, self.recv = part, box, send, recv

    def copy(self, direction, message, dest, src=None):
        d = 0 if direction == self.far else 1
        return remote(
            self.part((dest + 8) % 8) if src is None else src,
            self.box.at[d, message],
            self.send.at[d, message],
            self.recv.at[d, message],
            self.neighbour(direction),
        )

    def stage(self, st):
        odd = (st - 1) % 2

        @pl.when(self.delta == odd)
        def _():
            for direction in (self.far, -self.far):
                first = 1 if direction == self.far else 2
                if st < first:
                    continue
                d = 0 if direction == self.far else 1
                dest = self.place + direction * (5 - st)
                src = None
                if st > first:
                    message = (st - 2) // 2
                    self.copy(direction, message, dest).wait_recv()
                    src = self.box.at[d, message]
                    src[...] = src[...] + self.part((dest + 8) % 8)[...]
                self.copy(direction, (st - 1) // 2, dest, src).start()

    def last(self, out):
        @pl.when(self.delta == 0)
        def _():
            for direction in (self.far, -self.far):
                self.copy(direction, 1, self.place).wait_recv()
            out[...] = self.part(self.place)[...] + (self.box[0, 1] + self.box[1, 1])

    def finish(self):
        for direction in (self.far, -self.far):
            for message in range(2):
                first = 1 if direction == self.far else 2
                for odd in range(2):
                    stages = [
                        st for st in range(first, 5)
                        if (st - 1) % 2 == odd and (st - 1) // 2 == message
                    ]
                    if stages:

                        @pl.when(self.delta == odd)
                        def _():
                            self.copy(direction, message, self.place).wait_send()


def reduce_kernel(
    a_in, b_in, c_in, a_out, b_out, c_out,
    a_box, a_near, b_box, c_box, b_sum, c_sum, near_box, twin_box,
    c_send, c_recv, a_send, a_recv, n_send, n_recv, b_send, b_recv, f_send, f_recv,
):
    at = Place()
    mine = pl.ds(at.c * HALF, HALF)
    theirs = pl.ds((1 - at.c) * HALF, HALF)
    ring_c = RingReduce(
        at.z, at.delta_c, at.column, 1, lambda q: c_in.at[q // 2], c_box, c_send, c_recv
    )
    ring_a = RingReduce(
        at.s, at.delta_a, at.diagonal, -1, lambda q: a_near.at[q // 2], a_box, a_send, a_recv
    )
    near = remote(
        a_in.at[:, theirs], a_near, n_send.at[0], n_recv.at[0], at.other_core()
    )

    def straight_copy(step):
        y = (at.y + step) % 4
        return remote(
            b_in.at[y], b_box.at[at.y], b_send.at[step], b_recv.at[at.y], at.at(y=y)
        )

    def across_copy(y):
        return remote(
            b_in.at[y], b_box.at[at.y], b_send.at[y], b_recv.at[at.y], at.across(-1, y)
        )

    def b_arrival(y):
        return remote(b_in.at[y], b_box.at[y], b_send.at[0], b_recv.at[y], at.other_core())

    greet(at, twin=True, back=True)
    near.start()

    @pl.when(at.straight)
    def _():
        for step in range(1, 4):
            straight_copy(step).start()

    @pl.when(jnp.logical_not(at.straight))
    def _():
        for y in range(4):
            across_copy(y).start()

    ring_c.stage(1)
    near.wait()
    for slot in range(4):
        a_near[slot] = a_near[slot] + a_in[slot, mine, :]
    ring_a.stage(1)
    for st in range(2, 5):
        ring_c.stage(st)
        ring_a.stage(st)
    ring_c.last(c_sum)
    ring_a.last(a_out.at[mine])

    @pl.when(at.straight)
    def _():
        b_sum[...] = b_in[at.y]
        for step in range(1, 4):
            straight_copy(step).wait_send()
            b_arrival((at.y + step) % 4).wait_recv()
            b_sum[...] = b_sum[...] + b_box[(at.y + step) % 4]

    @pl.when(jnp.logical_not(at.straight))
    def _():
        for y in range(4):
            across_copy(y).wait_send()
            b_arrival(y).wait_recv()
        b_sum[...] = (b_box[0] + b_box[1]) + (b_box[2] + b_box[3])

    ring_c.finish()
    ring_a.finish()

    near_b = remote(b_sum.at[theirs], near_box.at[0], f_send.at[0], f_recv.at[0], at.other_core())
    near_c = remote(c_sum.at[theirs], near_box.at[1], f_send.at[1], f_recv.at[1], at.other_core())
    near_b.start()

    @pl.when(at.delta_c == 0)
    def _():
        near_c.start()
        c_out[mine, :] = c_sum[mine, :]

    @pl.when(at.delta_c == 1)
    def _():
        near_c.wait_recv()
        c_out[mine, :] = near_box[1]

    near_b.wait()
    b_out[mine, :] = b_sum[mine, :] + near_box[0]

    far_b = remote(b_out.at[mine], twin_box.at[0], f_send.at[2], f_recv.at[2], at.twin())
    far_c = remote(c_out.at[mine], twin_box.at[1], f_send.at[3], f_recv.at[3], at.twin())
    far_a = remote(a_out.at[mine], a_out.at[mine], f_send.at[4], f_recv.at[4], at.twin())
    far_b.start()
    far_c.start()

    @pl.when(at.delta_a == 0)
    def _():
        far_a.start()

    @pl.when(at.delta_c == 0)
    def _():
        near_c.wait_send()

    def last(ref, i):
        return remote(ref.at[mine], ref.at[mine], f_send.at[i], f_recv.at[i], at.other_core())

    def last_arrival(ref, i):
        return remote(ref.at[theirs], ref.at[theirs], f_send.at[i], f_recv.at[i], at.other_core())

    far_b.wait()
    b_out[mine, :] = b_out[mine, :] + twin_box[0]
    last(b_out, 5).start()
    far_c.wait()
    c_out[mine, :] = c_out[mine, :] + twin_box[1]
    last(c_out, 6).start()

    @pl.when(at.delta_a == 0)
    def _():
        far_a.wait_send()

    @pl.when(at.delta_a == 1)
    def _():
        far_a.wait_recv()

    last(a_out, 7).start()
    for i, ref in ((5, b_out), (6, c_out), (7, a_out)):
        last(ref, i).wait_send()
        last_arrival(ref, i).wait_recv()


def reduce(a, b, c):
    vmem = pl.BlockSpec(memory_space=pltpu.VMEM)
    out = jax.ShapeDtypeStruct((ROWS, WIDTH), jnp.float32)
    dma = pltpu.SemaphoreType.DMA
    f32 = jnp.float32
    return pl.pallas_call(
        reduce_kernel,
        out_shape=(out, out, out),
        in_specs=[vmem] * 3,
        out_specs=(vmem, vmem, vmem),
        scratch_shapes=[
            pltpu.VMEM((2, 2, HALF, WIDTH), f32),
            pltpu.VMEM((4, HALF, WIDTH), f32),
            pltpu.VMEM((4, ROWS, WIDTH), f32),
            pltpu.VMEM((2, 2, ROWS, WIDTH), f32),
            pltpu.VMEM((ROWS, WIDTH), f32),
            pltpu.VMEM((ROWS, WIDTH), f32),
            pltpu.VMEM((2, HALF, WIDTH), f32),
            pltpu.VMEM((2, HALF, WIDTH), f32),
            dma((2, 2)), dma((2, 2)), dma((2, 2)), dma((2, 2)),
            dma((1,)), dma((1,)), dma((4,)), dma((4,)), dma((8,)), dma((8,)),
        ],
        compiler_params=pltpu.CompilerParams(
            collective_id=1, has_side_effects=True, vmem_limit_bytes=56 << 20
        ),
    )(a, b, c)


def body(event, lidar, frame, sample_ids, logit_scale, logit_bias):
    at = Place()
    blocked = sample_ids.reshape(3, 64, ROWS)

    def ids(which, shards):
        return jnp.concatenate(
            [lax.dynamic_slice(blocked, (which, d, 0), (1, 1, ROWS)).reshape(ROWS) for d in shards]
        )

    first = (at.z - at.s + 8) % 8
    a_shards = []
    for slot in range(4):
        s = 2 * slot + at.xh
        y = jnp.where(s < 4, s, 7 - s)
        a_shards.append((s // 4) * 32 + y * 8 + (first + s) % 8)
    b_shards = [at.c * 32 + y * 8 + at.z for y in range(4)]
    parity = (at.c + at.xh) % 2
    c_shards = [at.xl * 32 + at.y * 8 + 2 * slot + parity for slot in range(4)]

    a, b, c = (m.reshape(BLOCK, WIDTH) for m in gather(event, lidar, frame))
    parts = compute(
        logit_scale, logit_bias, ids(0, a_shards), ids(1, b_shards), ids(2, c_shards), a, b, c
    )
    return reduce(*(g.reshape(4, ROWS, WIDTH) for g in parts))


def solution(mesh):
    placed = (P("dp", None), P("dp", None), P("dp", None), P(), P(), P())
    return jax.shard_map(
        body,
        mesh=mesh,
        in_specs=placed,
        out_specs=(P("dp", None), P("dp", None), P("dp", None)),
        check_vma=False,
    )
```

```python
import math

import jax
import jax.numpy as jnp
from jax import lax
from jax.experimental import pallas as pl
from jax.experimental.pallas import tpu as pltpu
from jax.sharding import PartitionSpec as P

MESH = pl.DeviceIdType.MESH
ROWS = 192
HALF = 96
QUARTER = 48
WIDTH = 1024
BLOCK = 768
TILE = 256
LOG2E = math.log2(math.e)
OFFSETS = {8: (4, 3, -3, 2, -2, 1, -1, 0), 4: (2, 1, -1, 0)}


class Place:
    def __init__(self):
        dp, group = lax.axis_index("dp"), lax.axis_index("group")
        self.xl, self.y, self.z = dp // 32, (dp // 8) % 4, dp % 8
        self.xh, self.c = group // 2, group % 2
        self.s = jnp.where(self.xl == 0, self.y, 7 - self.y)

    def at(self, xh=None, xl=None, y=None, z=None, c=None):
        xh, xl = self.xh if xh is None else xh, self.xl if xl is None else xl
        y, z = self.y if y is None else y, self.z if z is None else z
        c = self.c if c is None else c
        return (xl * 32 + y * 8 + z, xh * 2 + c)

    def column(self, step):
        return self.at(z=(self.z + step + 8) % 8)

    def row(self, step):
        return self.at(y=(self.y + step + 4) % 4)

    def diagonal(self, step):
        s = (self.s + step + 8) % 8
        return self.at(
            xl=s // 4, y=jnp.where(s < 4, s, 7 - s), z=(self.z + step + 8) % 8
        )

    def beside(self):
        return self.at(xl=1 - self.xl)

    def other_core(self):
        return self.at(c=1 - self.c)

    def twin(self, other=False):
        return self.at(xh=1 - self.xh, c=1 - self.c if other else self.c)


def remote(src, dst, send, recv, device):
    return pltpu.make_async_remote_copy(
        src_ref=src,
        dst_ref=dst,
        send_sem=send,
        recv_sem=recv,
        device_id=device,
        device_id_type=MESH,
    )


def slot(n, offset):
    return OFFSETS[n].index(n // 2 if offset == -(n // 2) else offset)


class RingGather:
    def __init__(self, n, neighbour, far, own, view, send, recv):
        self.n, self.neighbour, self.far, self.own = n, neighbour, far, own
        self.view, self.send, self.recv = view, send, recv

    def reach(self, direction):
        return self.n // 2 if direction == self.far else self.n // 2 - 1

    def copy(self, direction, step):
        d = 0 if direction == self.far else 1
        src = self.own if step == 1 else self.view(slot(self.n, -direction * (step - 1)))
        return remote(
            src,
            self.view(slot(self.n, -direction * step)),
            self.send.at[d, step - 1],
            self.recv.at[d, step - 1],
            self.neighbour(direction),
        )

    def start(self):
        for direction in (self.far, -self.far):
            self.copy(direction, 1).start()

    def stage(self, step, arrived=None):
        for direction in (self.far, -self.far):
            if step <= self.reach(direction):
                self.copy(direction, step).wait_recv()
                if step < self.reach(direction):
                    self.copy(direction, step + 1).start()
                if arrived is not None:
                    arrived(slot(self.n, -direction * step))

    def finish(self):
        for direction in (self.far, -self.far):
            for step in range(1, self.reach(direction) + 1):
                self.copy(direction, step).wait_send()


class Parcel:
    def __init__(self, out, out_scale, into, into_scale, send, recv, device):
        self.out, self.out_scale = out, out_scale
        self.into, self.into_scale = into, into_scale
        self.data = remote(out, into, send.at[0], recv.at[0], device)
        self.scale = remote(out_scale, into_scale, send.at[1], recv.at[1], device)

    def pack(self, value):
        top = jnp.max(jnp.abs(value), axis=0, keepdims=True)
        top = jnp.maximum(jnp.max(top, axis=1, keepdims=True), 1e-30)
        self.out[...] = (
            jnp.round(value * (32767.0 / top)).astype(jnp.int32).astype(jnp.int16)
        )
        self.out_scale[...] = jnp.broadcast_to(top * (1 / 32767.0), (8, 128))

    def start(self, value):
        self.pack(value)
        self.data.start()
        self.scale.start()

    def take(self):
        self.data.wait_recv()
        self.scale.wait_recv()
        return opened(self.into, self.into_scale)

    def sent(self):
        self.data.wait_send()
        self.scale.wait_send()


def opened(values, scale):
    return values[...].astype(jnp.int32).astype(jnp.float32) * scale[0:1, 0:1]


class RingReduce:
    def __init__(self, n, neighbour, far, part, box):
        self.n, self.neighbour, self.far, self.part, self.box = n, neighbour, far, part, box

    def parcel(self, direction, stage):
        out, out_scale, into, into_scale, send, recv = self.box
        i = stage - 1 if direction == self.far else self.n // 2 + stage - 2
        return Parcel(
            out.at[i], out_scale.at[i], into.at[i], into_scale.at[i],
            send.at[i], recv.at[i], self.neighbour(direction),
        )

    def first(self, direction):
        return 1 if direction == self.far else 2

    def stage(self, st):
        for direction in (self.far, -self.far):
            if st < self.first(direction):
                continue
            value = self.part(slot(self.n, direction * (self.n // 2 + 1 - st)))
            if st > self.first(direction):
                value = value + self.parcel(direction, st - 1).take()
            self.parcel(direction, st).start(value)

    def last(self):
        value = self.part(slot(self.n, 0))
        for direction in (self.far, -self.far):
            value = value + self.parcel(direction, self.n // 2).take()
        return value

    def finish(self):
        for direction in (self.far, -self.far):
            for st in range(self.first(direction), self.n // 2 + 1):
                self.parcel(direction, st).sent()


def greet(at):
    barrier = pltpu.get_barrier_semaphore()
    others = [at.column(-1), at.column(1), at.diagonal(-1), at.diagonal(1), at.row(-1), at.row(1)]
    others += [at.beside(), at.other_core(), at.twin(), at.twin(True)]
    for device in others:
        pl.semaphore_signal(barrier, inc=1, device_id=device, device_id_type=MESH)
    pl.semaphore_wait(barrier, len(others))


def coefficients(rows, cols, row_ids, col_ids, scale, bias):
    logits = lax.dot_general(
        rows, cols, (((1,), (1,)), ((), ())), preferred_element_type=jnp.float32
    )
    power = jnp.minimum(logits * (scale * -LOG2E) - bias * LOG2E, 126.0)
    sigmoid = 1.0 / (1.0 + jnp.exp2(power))
    label = jnp.where(row_ids == col_ids, 1.0, 0.0)
    return (sigmoid - label).astype(jnp.bfloat16)


def product(coef, rows):
    return jnp.dot(coef, rows, preferred_element_type=jnp.float32)


def product_t(coef, rows):
    return lax.dot_general(
        coef, rows, (((0,), (0,)), ((), ())), preferred_element_type=jnp.float32
    )


def kernel(
    scale, bias, a_col, a_row, b_row, c_col, a_own, b_own, c_own, a_out, b_out, c_out,
    a, b, c, ga, gb, gc, coef_ab, coef_ca, coef_cb,
    a_near, a_box, a_box_scale, b_box, b_box_scale, c_box, c_box_scale, e_box, e_box_scale, sums,
    ga_send, ga_recv, gb_send, gb_recv, gc_send, gc_recv, gt_send, gt_recv, gx_send, gx_recv, own_sem,
    ra_send, ra_recv, rb_send, rb_recv, rc_send, rc_recv, rt_send, rt_recv, re_send, re_recv, rf_send, rf_recv,
):
    at = Place()

    def span(start, size):
        return pl.ds(pl.multiple_of(start, 16), size)

    k = (at.c + at.xh) % 2
    my_b, my_c, my_a = span(at.c * HALF, HALF), span(k * HALF, HALF), span(at.xh * HALF, HALF)
    my_quarter = span(at.xh * HALF + at.c * QUARTER, QUARTER)

    def a_quarter(i, core):
        return a.at[span(i * HALF + core * QUARTER, QUARTER)]

    def piece(ref, i):
        return ref.at[i * HALF : (i + 1) * HALF]

    ring_c = RingGather(8, at.column, 1, c_own.at[my_c], lambda i: piece(c, i), gc_send, gc_recv)
    ring_a = RingGather(8, at.diagonal, -1, a_own.at[my_quarter], lambda i: a_quarter(i, at.c), ga_send, ga_recv)
    ring_b = [
        RingGather(4, at.row, 1, b_own.at[my_b], lambda i: piece(b, i), gb_send.at[0], gb_recv.at[0]),
        RingGather(4, at.row, -1, piece(b, 7), lambda i: piece(b, 4 + i), gb_send.at[1], gb_recv.at[1]),
    ]
    beside = remote(b_own.at[my_b], piece(b, 7), gx_send.at[0], gx_recv.at[0], at.beside())
    own = [
        pltpu.make_async_copy(a_own.at[my_a], piece(a, 7), own_sem.at[0]),
        pltpu.make_async_copy(b_own.at[my_b], piece(b, 3), own_sem.at[1]),
        pltpu.make_async_copy(c_own.at[my_c], piece(c, 7), own_sem.at[2]),
    ]

    def pass_over(i, core):
        view = a_quarter(i, core)
        return remote(view, view, gt_send.at[i], gt_recv.at[i], at.other_core())

    greet(at)
    ring_a.start()
    beside.start()
    ring_b[0].start()
    ring_c.start()
    for copy in own:
        copy.start()

    def to_other(i):
        pass_over(i, at.c).start()

    ring_a.stage(1, to_other)
    beside.wait_recv()
    ring_b[1].start()
    ring_c.stage(1)
    ring_a.stage(2, to_other)
    ring_b[0].stage(1)
    ring_b[1].stage(1)
    ring_a.stage(3, to_other)
    ring_c.stage(2)
    ring_b[0].stage(2)
    ring_b[1].stage(2)
    ring_a.stage(4, to_other)
    for copy in own:
        copy.wait()
    for i in range(7):
        pass_over(i, 1 - at.c).wait_recv()

    def ab_rows(i):
        rows = pl.ds(i * TILE, TILE)
        tile = coefficients(a[rows, :], b[...], a_col[rows, :], b_row[...], scale[0], bias[0])
        coef_ab[rows, :] = tile
        ga[rows, :] = scale[0] * product(tile, b[...])

    ab_rows(0)
    ring_c.stage(3)
    ab_rows(1)
    ab_rows(2)
    ring_c.stage(4)
    for i in range(BLOCK // TILE):
        cols = pl.ds(i * TILE, TILE)
        gb[cols, :] = scale[0] * product_t(coef_ab[:, cols], a[...])

    reduce_a = RingReduce(
        8, at.diagonal, -1,
        lambda i: ga[pl.ds(pl.multiple_of(i * HALF + at.c * QUARTER, 8), QUARTER), :] + a_near[i],
        (a_box.at[0], a_box_scale.at[0], a_box.at[1], a_box_scale.at[1], ra_send, ra_recv),
    )
    reduce_c = RingReduce(
        8, at.column, 1, lambda i: gc[i * HALF : (i + 1) * HALF, :],
        (c_box.at[0], c_box_scale.at[0], c_box.at[1], c_box_scale.at[1], rc_send, rc_recv),
    )
    reduce_b = [
        RingReduce(
            4, at.row, 1 - 2 * r, lambda i, r=r: gb[(4 * r + i) * HALF : (4 * r + i + 1) * HALF, :],
            (b_box.at[0, r], b_box_scale.at[0, r], b_box.at[1, r], b_box_scale.at[1, r], rb_send.at[r], rb_recv.at[r]),
        )
        for r in range(2)
    ]

    for g in range(4):
        rows = pl.ds(g * ROWS, ROWS)
        tile_a = coefficients(c[rows, :], a[...], c_col[rows, :], a_row[...], scale[1], bias[1])
        tile_b = coefficients(c[rows, :], b[...], c_col[rows, :], b_row[...], scale[2], bias[2])
        coef_ca[rows, :] = tile_a
        coef_cb[rows, :] = tile_b
        gc[rows, :] = scale[1] * product(tile_a, a[...]) + scale[2] * product(tile_b, b[...])
        reduce_c.stage(g + 1)

    def near(i, core):
        return remote(
            ga.at[pl.ds(pl.multiple_of(i * HALF + core * QUARTER, 8), QUARTER)], a_near.at[i],
            rt_send.at[i], rt_recv.at[i], at.other_core(),
        )

    for i in range(BLOCK // TILE):
        cols = pl.ds(i * TILE, TILE)
        ga[cols, :] = ga[cols, :] + scale[1] * product_t(coef_ca[:, cols], c[...])
    for i in range(8):
        near(i, 1 - at.c).start()
    for i in range(BLOCK // TILE):
        cols = pl.ds(i * TILE, TILE)
        gb[cols, :] = gb[cols, :] + scale[2] * product_t(coef_cb[:, cols], c[...])
    near(0, 1 - at.c).wait_recv()
    reduce_a.stage(1)
    for r in range(2):
        reduce_b[r].stage(1)
    for i in range(1, 8):
        near(i, 1 - at.c).wait_recv()

    out_e, out_e_scale = e_box.at[0], e_box_scale.at[0]
    in_e, in_e_scale = e_box.at[1], e_box_scale.at[1]

    def extra(i, device, rows=HALF):
        return Parcel(
            out_e.at[i, 0:rows], out_e_scale.at[i], in_e.at[i, 0:rows], in_e_scale.at[i],
            re_send.at[i], re_recv.at[i], device,
        )

    twin_c = extra(0, at.twin(True))
    beside_b = extra(1, at.beside())
    twin_b = extra(2, at.twin())
    twin_a = extra(3, at.twin(), QUARTER)

    def to_core(out, rows, i):
        return remote(out.at[rows], out.at[rows], rf_send.at[i], rf_recv.at[i], at.other_core())

    def settle(parcel, out, rows, i):
        mine = opened(parcel.out, parcel.out_scale)
        out[rows, :] = mine + parcel.take()
        to_core(out, rows, i).start()

    reduce_a.stage(2)
    for r in range(2):
        reduce_b[r].stage(2)
    twin_c.start(reduce_c.last())
    reduce_a.stage(3)
    sums[...] = reduce_b[0].last()
    beside_b.start(reduce_b[1].last())
    reduce_a.stage(4)
    settle(twin_c, c_out, my_c, 0)
    twin_b.start(sums[...] + beside_b.take())
    twin_a.start(reduce_a.last())
    a_out[my_quarter, :] = opened(twin_a.out, twin_a.out_scale)
    to_core(a_out, my_quarter, 2).start()
    settle(twin_b, b_out, my_b, 1)
    far_quarter = span((1 - at.xh) * HALF + at.c * QUARTER, QUARTER)
    a_out[far_quarter, :] = twin_a.take()
    to_core(a_out, far_quarter, 3).start()

    for ring in (ring_a, ring_c, *ring_b, reduce_a, reduce_c, *reduce_b):
        ring.finish()
    beside.wait_send()
    for i in range(7):
        pass_over(i, at.c).wait_send()
    for i in range(8):
        near(i, 1 - at.c).wait_send()
    for parcel in (twin_a, twin_b, twin_c, beside_b):
        parcel.sent()
    for out, rows, other_rows, i in (
        (c_out, my_c, span((1 - k) * HALF, HALF), 0),
        (b_out, my_b, span((1 - at.c) * HALF, HALF), 1),
        (a_out, my_quarter, span(at.xh * HALF + (1 - at.c) * QUARTER, QUARTER), 2),
        (a_out, far_quarter, span((1 - at.xh) * HALF + (1 - at.c) * QUARTER, QUARTER), 3),
    ):
        to_core(out, rows, i).wait_send()
        to_core(out, other_rows, i).wait_recv()


def gradients(scale, bias, a_ids, b_ids, c_ids, a, b, c):
    vmem = pl.BlockSpec(memory_space=pltpu.VMEM)
    smem = pl.BlockSpec(memory_space=pltpu.SMEM)
    hbm = pl.BlockSpec(memory_space=pl.ANY)
    out = jax.ShapeDtypeStruct((ROWS, WIDTH), jnp.float32)
    dma = pltpu.SemaphoreType.DMA
    f32, bf16, i16 = jnp.float32, jnp.bfloat16, jnp.int16
    m = pltpu.VMEM
    return pl.pallas_call(
        kernel,
        out_shape=(out, out, out),
        in_specs=[smem, smem] + [vmem] * 4 + [hbm] * 3,
        out_specs=(vmem, vmem, vmem),
        scratch_shapes=[
            m((BLOCK, WIDTH), bf16), m((BLOCK, WIDTH), bf16), m((BLOCK, WIDTH), bf16),
            m((BLOCK, WIDTH), f32), m((BLOCK, WIDTH), f32), m((BLOCK, WIDTH), f32),
            m((BLOCK, BLOCK), bf16), m((BLOCK, BLOCK), bf16), m((BLOCK, BLOCK), bf16),
            m((8, QUARTER, WIDTH), f32),
            m((2, 7, QUARTER, WIDTH), i16), m((2, 7, 8, 128), f32),
            m((2, 2, 3, HALF, WIDTH), i16), m((2, 2, 3, 8, 128), f32),
            m((2, 7, HALF, WIDTH), i16), m((2, 7, 8, 128), f32),
            m((2, 4, HALF, WIDTH), i16), m((2, 4, 8, 128), f32),
            m((HALF, WIDTH), f32),
            dma((2, 4)), dma((2, 4)), dma((2, 2, 2)), dma((2, 2, 2)), dma((2, 4)), dma((2, 4)),
            dma((7,)), dma((7,)), dma((1,)), dma((1,)), dma((3,)),
            dma((7, 2)), dma((7, 2)), dma((2, 3, 2)), dma((2, 3, 2)), dma((7, 2)), dma((7, 2)),
            dma((8,)), dma((8,)), dma((4, 2)), dma((4, 2)), dma((4,)), dma((4,)),
        ],
        compiler_params=pltpu.CompilerParams(
            collective_id=0, has_side_effects=True, vmem_limit_bytes=56 << 20
        ),
    )(
        scale, bias, a_ids.reshape(BLOCK, 1), a_ids.reshape(1, BLOCK),
        b_ids.reshape(1, BLOCK), c_ids.reshape(BLOCK, 1), a, b, c,
    )


def body(event, lidar, frame, sample_ids, logit_scale, logit_bias):
    at = Place()
    blocked = sample_ids.reshape(3, 64, 2, HALF)

    def ids(which, half, shards):
        return jnp.concatenate(
            [lax.dynamic_slice(blocked, (which, d, half, 0), (1, 1, 1, HALF)).reshape(HALF) for d in shards]
        )

    def diagonal(o):
        s = (at.s + o + 8) % 8
        return at.at(xl=s // 4, y=jnp.where(s < 4, s, 7 - s), z=(at.z + o + 8) % 8)[0]

    a_ids = ids(0, at.xh, [diagonal(o) for o in OFFSETS[8]])
    b_ids = ids(1, at.c, [at.at(xl=xl, y=(at.y + o + 4) % 4)[0] for xl in (at.xl, 1 - at.xl) for o in OFFSETS[4]])
    c_ids = ids(2, (at.c + at.xh) % 2, [at.at(z=(at.z + o + 8) % 8)[0] for o in OFFSETS[8]])
    return gradients(logit_scale, logit_bias, a_ids, b_ids, c_ids, event, lidar, frame)


def solution(mesh):
    placed = (P("dp", None), P("dp", None), P("dp", None), P(), P(), P())
    return jax.shard_map(
        body,
        mesh=mesh,
        in_specs=placed,
        out_specs=(P("dp", None), P("dp", None), P("dp", None)),
        check_vma=False,
    )
```

```python
import math

import jax
import jax.numpy as jnp
from jax import lax
from jax.experimental import pallas as pl
from jax.experimental.pallas import tpu as pltpu
from jax.sharding import PartitionSpec as P

MESH = pl.DeviceIdType.MESH
ROWS = 192
HALF = 96
QUARTER = 48
WIDTH = 1024
BLOCK = 768
TOKENS = 12288
TILE = 256
LOG2E = math.log2(math.e)
OFFSETS = {8: (4, 3, -3, 2, -2, 1, -1, 0), 4: (2, 1, -1, 0)}

ORDER = (
    "sP", "sA", "sC", "sX", "X", "C1", "A1", "A2", "Q1", "C2", "P1", "C3", "A3", "cb2", "ab3", "cb3",
    "A4", "C4", "ab2", "ab1", "ab0", "cb1", "ca1", "c0n1", "cb0", "c1n1", "ca0", "c1f1", "bc0", "ca3",
    "c0f1", "bc1", "b0f1", "b0n1", "ca2", "ac0", "c1f2", "ns0", "c1n2", "an1", "c0f2", "ac1", "af1",
    "b1f1", "ns1", "c0n2", "ac2", "bc2", "b0f2", "c1f3", "c0f3", "ns2", "b1n1", "af2", "c1f4", "b1f2",
    "c1n3", "Lb0", "xf1", "c0n3", "an2", "c0f4", "Lc1", "af3", "Lb1", "xn1", "xf2", "af4", "an3", "Lc0",
    "Sc1", "Lx", "La", "Ob", "Sc0", "Oa",
)


class Place:
    def __init__(self):
        dp, group = lax.axis_index("dp"), lax.axis_index("group")
        self.xl, self.y, self.z = dp // 32, (dp // 8) % 4, dp % 8
        self.xh, self.c = group // 2, group % 2
        self.s = jnp.where(self.xl == 0, self.y, 7 - self.y)

    def at(self, xh=None, xl=None, y=None, z=None, c=None):
        xh, xl = self.xh if xh is None else xh, self.xl if xl is None else xl
        y, z = self.y if y is None else y, self.z if z is None else z
        c = self.c if c is None else c
        return (xl * 32 + y * 8 + z, xh * 2 + c)

    def column(self, step):
        return self.at(z=(self.z + step + 8) % 8)

    def row(self, step):
        return self.at(y=(self.y + step + 4) % 4)

    def diagonal(self, step):
        s = (self.s + step + 8) % 8
        return self.at(
            xl=s // 4, y=jnp.where(s < 4, s, 7 - s), z=(self.z + step + 8) % 8
        )

    def line(self, step):
        x = (self.xh * 2 + self.xl + step + 4) % 4
        return self.at(xh=x // 2, xl=x % 2)

    def beside(self):
        return self.at(xl=1 - self.xl)

    def other_core(self):
        return self.at(c=1 - self.c)

    def twin(self, other=False):
        return self.at(xh=1 - self.xh, c=1 - self.c if other else self.c)


def remote(src, dst, send, recv, device):
    return pltpu.make_async_remote_copy(
        src_ref=src,
        dst_ref=dst,
        send_sem=send,
        recv_sem=recv,
        device_id=device,
        device_id_type=MESH,
    )


def slot(n, offset):
    return OFFSETS[n].index(n // 2 if offset == -(n // 2) else offset)


class RingGather:
    def __init__(self, n, neighbour, far, own, view, send, recv):
        self.n, self.neighbour, self.far, self.own = n, neighbour, far, own
        self.view, self.send, self.recv = view, send, recv

    def reach(self, direction):
        return self.n // 2 if direction == self.far else self.n // 2 - 1

    def copy(self, direction, step):
        d = 0 if direction == self.far else 1
        src = self.own if step == 1 else self.view(slot(self.n, -direction * (step - 1)))
        return remote(
            src,
            self.view(slot(self.n, -direction * step)),
            self.send.at[d, step - 1],
            self.recv.at[d, step - 1],
            self.neighbour(direction),
        )

    def start(self):
        for direction in (self.far, -self.far):
            self.copy(direction, 1).start()

    def stage(self, step, arrived=None):
        for direction in (self.far, -self.far):
            if step <= self.reach(direction):
                self.copy(direction, step).wait_recv()
                if step < self.reach(direction):
                    self.copy(direction, step + 1).start()
                if arrived is not None:
                    arrived(slot(self.n, -direction * step))

    def finish(self):
        for direction in (self.far, -self.far):
            for step in range(1, self.reach(direction) + 1):
                self.copy(direction, step).wait_send()


class Parcel:
    def __init__(self, out, out_scale, into, into_scale, send, recv, device):
        self.out, self.out_scale = out, out_scale
        self.into, self.into_scale = into, into_scale
        self.data = remote(out, into, send.at[0], recv.at[0], device)
        self.scale = remote(out_scale, into_scale, send.at[1], recv.at[1], device)

    def pack(self, value):
        top = jnp.max(jnp.abs(value), axis=0, keepdims=True)
        top = jnp.maximum(jnp.max(top, axis=1, keepdims=True), 1e-30)
        self.out[...] = (
            jnp.round(value * (32767.0 / top)).astype(jnp.int32).astype(jnp.int16)
        )
        self.out_scale[...] = jnp.broadcast_to(top * (1 / 32767.0), (8, 128))

    def go(self):
        self.data.start()
        self.scale.start()

    def start(self, value):
        self.pack(value)
        self.go()

    def arrive(self):
        self.data.wait_recv()
        self.scale.wait_recv()

    def take(self):
        self.arrive()
        return self.into[...].astype(jnp.int32).astype(jnp.float32) * self.into_scale[0:1, 0:1]

    def sent(self):
        self.data.wait_send()
        self.scale.wait_send()


class RingReduce:
    def __init__(self, n, neighbour, far, part, box):
        self.n, self.neighbour, self.far, self.part, self.box = n, neighbour, far, part, box

    def steps(self, direction):
        return self.n // 2 if direction == self.far else self.n // 2 - 1

    def parcel(self, direction, step):
        out, out_scale, into, into_scale, send, recv = self.box
        i = step - 1 if direction == self.far else self.n // 2 + step - 1
        return Parcel(
            out.at[i], out_scale.at[i], into.at[i], into_scale.at[i],
            send.at[i], recv.at[i], self.neighbour(direction),
        )

    def step(self, direction, step):
        if step > self.steps(direction):
            return
        value = self.part(slot(self.n, direction * (self.steps(direction) + 1 - step)))
        if step > 1:
            value = value + self.parcel(direction, step - 1).take()
        self.parcel(direction, step).start(value)

    def both(self, step):
        self.step(self.far, step)
        self.step(-self.far, step)

    def last(self):
        value = self.part(slot(self.n, 0))
        for direction in (self.far, -self.far):
            value = value + self.parcel(direction, self.steps(direction)).take()
        return value

    def finish(self):
        for direction in (self.far, -self.far):
            for step in range(1, self.steps(direction) + 1):
                self.parcel(direction, step).sent()


def greet(at, meanwhile):
    barrier = pltpu.get_barrier_semaphore()
    others = [at.column(-1), at.column(1), at.diagonal(-1), at.diagonal(1), at.row(-1), at.row(1)]
    others += [at.line(-1), at.line(1), at.other_core(), at.twin(), at.twin(True)]
    for device in others:
        pl.semaphore_signal(barrier, inc=1, device_id=device, device_id_type=MESH)
    meanwhile()
    pl.semaphore_wait(barrier, len(others))


def coefficients(rows, cols, row_ids, col_ids, scale, bias):
    logits = lax.dot_general(
        rows, cols, (((1,), (1,)), ((), ())), preferred_element_type=jnp.float32
    )
    power = jnp.minimum(logits * (scale * -LOG2E) - bias * LOG2E, 126.0)
    sigmoid = 1.0 / (1.0 + jnp.exp2(power))
    label = jnp.where(row_ids == col_ids, 1.0, 0.0)
    return (sigmoid - label).astype(jnp.bfloat16)


def product(coef, rows):
    return jnp.dot(coef, rows, preferred_element_type=jnp.float32)


def product_t(coef, rows):
    return lax.dot_general(
        coef, rows, (((0,), (0,)), ((), ())), preferred_element_type=jnp.float32
    )


def kernel(
    scale, bias, all_ids, a_own, b_own, c_own, a_out, b_out, c_out, a_unit, b_unit, c_unit, ids, ids_t,
    a, b, c, ga, gb, gc, coef_ab, coef_ca, coef_cb,
    a_near, a_box, a_box_scale, b_box, b_box_scale, c_box, c_box_scale, x_box, x_box_scale, sums,
    ga_send, ga_recv, gb_send, gb_recv, gc_send, gc_recv, gt_send, gt_recv, gx_send, gx_recv, gw_send, gw_recv, own_sem,
    ra_send, ra_recv, rb_send, rb_recv, rc_send, rc_recv, rx_send, rx_recv, rt_send, rt_recv, re_send, re_recv,
):
    at = Place()

    def span(start, size):
        return pl.ds(pl.multiple_of(start, 16), size)

    k = (at.c + at.xh) % 2
    my_b, my_c, my_a = span(at.c * HALF, HALF), span(k * HALF, HALF), span(at.xh * HALF, HALF)
    my_quarter = span(at.xh * HALF + at.c * QUARTER, QUARTER)

    def a_quarter(i, core):
        return a.at[span(i * HALF + core * QUARTER, QUARTER)]

    def piece(ref, i):
        return ref.at[i * HALF : (i + 1) * HALF]

    def c_quarter(i, part):
        return c.at[span(i * HALF + part * QUARTER, QUARTER)]

    my_part = span(k * HALF + at.xh * QUARTER, QUARTER)
    ring_c = RingGather(8, at.column, 1, c_own.at[my_part], lambda i: c_quarter(i, at.xh), gc_send, gc_recv)
    ring_a = RingGather(8, at.diagonal, -1, a_own.at[my_quarter], lambda i: a_quarter(i, at.c), ga_send, ga_recv)
    ring_b = [
        RingGather(4, at.row, 1, b_own.at[my_b], lambda i: piece(b, i), gb_send.at[0], gb_recv.at[0]),
        RingGather(4, at.row, -1, piece(b, 7), lambda i: piece(b, 4 + i), gb_send.at[1], gb_recv.at[1]),
    ]
    beside = remote(b_own.at[my_b], piece(b, 7), gx_send.at[0], gx_recv.at[0], at.beside())
    own = [
        pltpu.make_async_copy(a_own.at[my_a], piece(a, 7), own_sem.at[0]),
        pltpu.make_async_copy(b_own.at[my_b], piece(b, 3), own_sem.at[1]),
        pltpu.make_async_copy(c_own.at[my_c], piece(c, 7), own_sem.at[2]),
    ]

    def pass_over(i, core):
        view = a_quarter(i, core)
        return remote(view, view, gt_send.at[i], gt_recv.at[i], at.other_core())

    def share(i, part):
        view = c_quarter(i, part)
        return remote(view, view, gw_send.at[i], gw_recv.at[i], at.twin(True))

    done = set()

    def once(key, wait):
        if key not in done:
            done.add(key)
            wait()

    def to_other(i):
        pass_over(i, at.c).start()

    def gather_a(step):
        ring_a.stage(step, to_other)

    def gather_c(step):
        ring_c.stage(step, lambda i: share(i, at.xh).start())

    def x_done():
        beside.wait_recv()
        ring_b[1].start()

    def a_here(*groups):
        once("own", lambda: [copy.wait() for copy in own])
        for i in (i for g in groups or range(4) for i in (2 * g, 2 * g + 1)):
            if i < 7:
                once(("a", i), lambda: pass_over(i, 1 - at.c).wait_recv())

    def b_here():
        once("own", lambda: [copy.wait() for copy in own])
        for r in range(2):
            once(("b", r), lambda: ring_b[r].stage(2))

    def c_here(g):
        once("own", lambda: [copy.wait() for copy in own])
        for i in (2 * g, 2 * g + 1):
            if i < 7:
                once(("c", i), lambda: share(i, 1 - at.xh).wait_recv())

    def ab_rows(g):
        a_here(g)
        b_here()
        rows = pl.ds(g * ROWS, ROWS)
        tile = coefficients(a[rows, :], b[...], ids_t[rows, 0:1], ids[1:2, 0:BLOCK], scale[0], bias[0])
        coef_ab[rows, :] = tile
        ga[rows, :] = scale[0] * product(tile, b[...])

    def cb_rows(g):
        b_here()
        c_here(g)
        rows = pl.ds(g * ROWS, ROWS)
        tile = coefficients(c[rows, :], b[...], ids_t[rows, 2:3], ids[1:2, 0:BLOCK], scale[2], bias[2])
        coef_cb[rows, :] = tile
        gc[rows, :] = scale[2] * product(tile, b[...])

    def ca_rows(g):
        a_here()
        c_here(g)
        rows = pl.ds(g * ROWS, ROWS)
        tile = coefficients(c[rows, :], a[...], ids_t[rows, 2:3], ids[0:1, 0:BLOCK], scale[1], bias[1])
        coef_ca[rows, :] = tile
        gc[rows, :] = gc[rows, :] + scale[1] * product(tile, a[...])

    def a_cols(i):
        cols = pl.ds(i * TILE, TILE)
        ga[cols, :] = ga[cols, :] + scale[1] * product_t(coef_ca[:, cols], c[...])

    def b_cols(i):
        cols = pl.ds(i * TILE, TILE)
        gb[cols, :] = scale[0] * product_t(coef_ab[:, cols], a[...]) + scale[2] * product_t(coef_cb[:, cols], c[...])

    def a_part(i):
        once(("near", i), lambda: near(i, 1 - at.c).wait_recv())
        return ga[pl.ds(pl.multiple_of(i * HALF + at.c * QUARTER, 8), QUARTER), :] + a_near[i]

    reduce_a = RingReduce(
        8, at.diagonal, -1, a_part,
        (a_box.at[0], a_box_scale.at[0], a_box.at[1], a_box_scale.at[1], ra_send, ra_recv),
    )

    def c_ring(q):
        def part(i):
            return gc[i * HALF + q * QUARTER : i * HALF + (q + 1) * QUARTER, :]

        return RingReduce(
            8, at.column, 1, part,
            (c_box.at[0, q], c_box_scale.at[0, q], c_box.at[1, q], c_box_scale.at[1, q], rc_send.at[q], rc_recv.at[q]),
        )

    reduce_c = [c_ring(q) for q in range(2)]
    reduce_b = [
        RingReduce(
            4, at.row, 1 - 2 * r, lambda i, r=r: gb[(4 * r + i) * HALF : (4 * r + i + 1) * HALF, :],
            (b_box.at[0, r], b_box_scale.at[0, r], b_box.at[1, r], b_box_scale.at[1, r], rb_send.at[r], rb_recv.at[r]),
        )
        for r in range(2)
    ]

    def x_part(i):
        next_part = (at.xh + at.xl) % 2
        r, part = ((0, 1 - at.xh), (1, next_part), (1, 1 - next_part), (0, at.xh))[i]
        return sums[r, pl.ds(pl.multiple_of(part * QUARTER, 8), QUARTER), :]

    reduce_x = RingReduce(
        4, at.line, 1, x_part,
        (x_box.at[0], x_box_scale.at[0], x_box.at[1], x_box_scale.at[1], rx_send, rx_recv),
    )

    def near(i, core):
        return remote(
            ga.at[pl.ds(pl.multiple_of(i * HALF + core * QUARTER, 8), QUARTER)], a_near.at[i],
            rt_send.at[i], rt_recv.at[i], at.other_core(),
        )

    def rows_of(half, part):
        return span(half * HALF + part * QUARTER, QUARTER)

    def ready(out, unit, half, part, i, device):
        rows, number = out.at[rows_of(half, part)], unit.at[2 * half + part]
        return Parcel(rows, number, rows, number, re_send.at[i], re_recv.at[i], device)

    def to_twin(i):
        if i < 2:
            return ready(c_out.at[at.xh], c_unit.at[at.xh], k, i, i, at.twin(True))
        if i == 2:
            return ready(b_out, b_unit, at.c, at.xh, i, at.twin())
        return ready(a_out, a_unit, at.xh, at.c, i, at.twin())

    def from_twin(i):
        if i < 2:
            return ready(c_out.at[1 - at.xh], c_unit.at[1 - at.xh], k, i, i, at.twin(True))
        if i == 2:
            return ready(b_out, b_unit, at.c, 1 - at.xh, i, at.twin())
        return ready(a_out, a_unit, 1 - at.xh, at.c, i, at.twin())

    def to_core(i, other):
        chip = 1 - at.xh if other else at.xh
        j = 4 + 2 * i + other
        if i < 2:
            return ready(c_out.at[chip], c_unit.at[chip], k, i, j, at.other_core())
        if i == 2:
            return ready(b_out, b_unit, at.c, chip, j, at.other_core())
        return ready(a_out, a_unit, chip, at.c, j, at.other_core())

    def from_core(i, other):
        chip = 1 - at.xh if other else at.xh
        j = 4 + 2 * i + other
        if i < 2:
            return ready(c_out.at[chip], c_unit.at[chip], 1 - k, i, j, at.other_core())
        if i == 2:
            return ready(b_out, b_unit, 1 - at.c, chip, j, at.other_core())
        return ready(a_out, a_unit, chip, 1 - at.c, j, at.other_core())

    def mine_done(i, value):
        to_twin(i).start(value)
        to_core(i, 0).go()

    def other_done(i):
        from_twin(i).arrive()
        to_core(i, 1).go()

    def near_go(i):
        for j in ((0, 1), (2, 3, 4), (5, 6, 7))[i]:
            near(j, 1 - at.c).start()

    def b_last(r):
        sums[r] = reduce_b[r].last()

    steps = {
        "sA": ring_a.start,
        "sC": ring_c.start,
        "sX": beside.start,
        "sP": ring_b[0].start,
        "X": x_done,
        "P1": lambda: ring_b[0].stage(1),
        "Q1": lambda: ring_b[1].stage(1),
        "La": lambda: mine_done(3, reduce_a.last()),
        "Lx": lambda: mine_done(2, reduce_x.last()),
        "Oa": lambda: other_done(3),
        "Ob": lambda: other_done(2),
    }
    for i in range(1, 5):
        steps[f"A{i}"] = lambda i=i: gather_a(i)
        steps[f"C{i}"] = lambda i=i: gather_c(i)
    for i in range(4):
        steps[f"ab{i}"] = lambda i=i: ab_rows(i)
        steps[f"cb{i}"] = lambda i=i: cb_rows(i)
        steps[f"ca{i}"] = lambda i=i: ca_rows(i)
    for i in range(3):
        steps[f"ac{i}"] = lambda i=i: a_cols(i)
        steps[f"bc{i}"] = lambda i=i: b_cols(i)
        steps[f"ns{i}"] = lambda i=i: near_go(i)
    for q in range(2):
        steps[f"Lb{q}"] = lambda q=q: b_last(q)
        steps[f"Lc{q}"] = lambda q=q: mine_done(q, reduce_c[q].last())
        steps[f"Sc{q}"] = lambda q=q: other_done(q)
    for name, ring in (("a", reduce_a), ("b0", reduce_b[0]), ("b1", reduce_b[1]), ("c0", reduce_c[0]), ("c1", reduce_c[1]), ("x", reduce_x)):
        for way, direction in (("f", ring.far), ("n", -ring.far)):
            for i in range(1, ring.steps(direction) + 1):
                steps[f"{name}{way}{i}"] = lambda ring=ring, d=direction, i=i: ring.step(d, i)

    def shards_of(which):
        if which == 0:
            return [at.diagonal(o)[0] for o in OFFSETS[8]], at.xh
        if which == 1:
            return [at.at(xl=xl, y=(at.y + o + 4) % 4)[0] for xl in (at.xl, 1 - at.xl) for o in OFFSETS[4]], at.c
        return [at.column(o)[0] for o in OFFSETS[8]], k

    def lay_out_ids():
        ids[...] = jnp.zeros_like(ids)
        lane = lax.broadcasted_iota(jnp.int32, (3, 256), 1)
        row = lax.broadcasted_iota(jnp.int32, (3, 256), 0)
        for which in range(3):
            shards, half = shards_of(which)
            for i, shard in enumerate(shards):
                base = shard * ROWS + half * HALF
                start = base // 128 * 128 - base // (TOKENS - HALF) * 128
                window = all_ids[:, pl.ds(pl.multiple_of(start, 128), 256)]
                first = i * HALF % 128
                moved = pltpu.roll(window, (first - base + start + 256) % 256, 1)
                here = (row == which) & (lane >= first) & (lane < first + HALF)
                place = (slice(0, 3), slice(i * HALF - first, i * HALF - first + 256))
                ids[place] = jnp.where(here, moved, ids[place])
        ids_t[...] = jnp.transpose(ids[:, 0:BLOCK])

    for copy in own:
        copy.start()
    greet(at, lay_out_ids)
    for name in ORDER:
        steps[name]()

    for ring in (ring_a, ring_c, *ring_b, reduce_a, reduce_x, *reduce_c, *reduce_b):
        ring.finish()
    beside.wait_send()
    for i in range(7):
        pass_over(i, at.c).wait_send()
        share(i, at.xh).wait_send()
    for i in range(8):
        near(i, 1 - at.c).wait_send()
    for i in range(4):
        to_twin(i).sent()
        for other in range(2):
            to_core(i, other).sent()
            from_core(i, other).arrive()


def gradients(scale, bias, ids, a, b, c):
    vmem = pl.BlockSpec(memory_space=pltpu.VMEM)
    smem = pl.BlockSpec(memory_space=pltpu.SMEM)
    hbm = pl.BlockSpec(memory_space=pl.ANY)
    dma = pltpu.SemaphoreType.DMA
    f32, bf16, i16 = jnp.float32, jnp.bfloat16, jnp.int16
    m = pltpu.VMEM
    shape = jax.ShapeDtypeStruct
    a, b, c, a_unit, b_unit, c_unit = pl.pallas_call(
        kernel,
        out_shape=(
            shape((ROWS, WIDTH), i16), shape((ROWS, WIDTH), i16), shape((2, ROWS, WIDTH), i16),
            shape((4, 8, 128), f32), shape((4, 8, 128), f32), shape((2, 4, 8, 128), f32),
        ),
        in_specs=[smem, smem, vmem] + [hbm] * 3,
        out_specs=(vmem,) * 6,
        scratch_shapes=[
            m((8, 896), jnp.int32), m((BLOCK, 8), jnp.int32),
            m((BLOCK, WIDTH), bf16), m((BLOCK, WIDTH), bf16), m((BLOCK, WIDTH), bf16),
            m((BLOCK, WIDTH), f32), m((BLOCK, WIDTH), f32), m((BLOCK, WIDTH), f32),
            m((BLOCK, BLOCK), bf16), m((BLOCK, BLOCK), bf16), m((BLOCK, BLOCK), bf16),
            m((8, QUARTER, WIDTH), f32),
            m((2, 7, QUARTER, WIDTH), i16), m((2, 7, 8, 128), f32),
            m((2, 2, 3, HALF, WIDTH), i16), m((2, 2, 3, 8, 128), f32),
            m((2, 2, 7, QUARTER, WIDTH), i16), m((2, 2, 7, 8, 128), f32),
            m((2, 3, QUARTER, WIDTH), i16), m((2, 3, 8, 128), f32),
            m((2, HALF, WIDTH), f32),
            dma((2, 4)), dma((2, 4)), dma((2, 2, 2)), dma((2, 2, 2)), dma((2, 4)), dma((2, 4)),
            dma((7,)), dma((7,)), dma((1,)), dma((1,)), dma((7,)), dma((7,)), dma((3,)),
            dma((7, 2)), dma((7, 2)), dma((2, 3, 2)), dma((2, 3, 2)), dma((2, 7, 2)), dma((2, 7, 2)), dma((3, 2)), dma((3, 2)),
            dma((8,)), dma((8,)), dma((12, 2)), dma((12, 2)),
        ],
        compiler_params=pltpu.CompilerParams(
            collective_id=0, has_side_effects=True, vmem_limit_bytes=56 << 20
        ),
    )(scale, bias, ids, a, b, c)
    return decode(a, b, c, a_unit, b_unit, c_unit)


def decode_kernel(a, b, c, a_unit, b_unit, c_unit, a_out, b_out, c_out):
    def value(code, unit):
        return code.astype(jnp.int32).astype(jnp.float32) * unit[0:1, 0:1]

    for i in range(4):
        rows = pl.ds(i * QUARTER, QUARTER)
        a_out[rows, :] = value(a[rows, :], a_unit[i])
        b_out[rows, :] = value(b[rows, :], b_unit[i])
        c_out[rows, :] = value(c[0, rows, :], c_unit[0, i]) + value(c[1, rows, :], c_unit[1, i])


def decode(a, b, c, a_unit, b_unit, c_unit):
    vmem = pl.BlockSpec(memory_space=pltpu.VMEM)
    out = jax.ShapeDtypeStruct((ROWS, WIDTH), jnp.float32)
    return pl.pallas_call(
        decode_kernel,
        out_shape=(out, out, out),
        in_specs=[vmem] * 6,
        out_specs=(vmem, vmem, vmem),
    )(a, b, c, a_unit, b_unit, c_unit)


def body(event, lidar, frame, sample_ids, logit_scale, logit_bias):
    return gradients(logit_scale, logit_bias, sample_ids, event, lidar, frame)


def solution(mesh):
    placed = (P("dp", None), P("dp", None), P("dp", None), P(), P(), P())
    return jax.shard_map(
        body,
        mesh=mesh,
        in_specs=placed,
        out_specs=(P("dp", None), P("dp", None), P("dp", None)),
        check_vma=False,
    )
```

```python
import math

import jax
import jax.numpy as jnp
from jax import lax
from jax.experimental import pallas as pl
from jax.experimental.pallas import tpu as pltpu
from jax.sharding import PartitionSpec as P

MESH = pl.DeviceIdType.MESH
ROWS = 192
HALF = 96
QUARTER = 48
WIDTH = 1024
BLOCK = 768
TOKENS = 12288
TILE = 256
LOG2E = math.log2(math.e)
OFFSETS = {8: (4, 3, -3, 2, -2, 1, -1, 0), 4: (2, 1, -1, 0)}

ORDER = (
    "sC", "sP", "sX", "sA", "sD", "P1", "D1", "C1", "P2", "A1", "C2", "A2", "ab2", "D2", "cb3", "A3",
    "C3", "ab3", "cb2", "ab1", "D3", "A4", "cb1", "C4", "ab0", "ca1", "D4", "cb0", "ca0", "c1f1", "bc1",
    "bc0", "x0f1", "c0f1", "c0n1", "bc2", "x0n1", "ca2", "c1f2", "ca3", "ac0", "c1n1", "x1f1", "ns0",
    "c0f2", "af1", "x0f2", "c1f3", "c0n2", "ac1", "c1n2", "ac2", "an1", "ns1", "c1f4", "af2", "Lx0",
    "yf1", "x1n1", "ns2", "c0f3", "x1f2", "c1n3", "an2", "af3", "c0n3", "c0f4", "yf2", "Lx1", "Lc1",
    "an3", "yn1", "af4", "Lc0", "Ly", "Sc1", "La", "Sc0", "Ob", "Oa",
)


class Place:
    def __init__(self):
        dp, group = lax.axis_index("dp"), lax.axis_index("group")
        self.xl, self.y, self.z = dp // 32, (dp // 8) % 4, dp % 8
        self.xh, self.c = group // 2, group % 2
        self.s = jnp.where(self.xl == 0, self.y, 7 - self.y)

    def at(self, xh=None, xl=None, y=None, z=None, c=None):
        xh, xl = self.xh if xh is None else xh, self.xl if xl is None else xl
        y, z = self.y if y is None else y, self.z if z is None else z
        c = self.c if c is None else c
        return (xl * 32 + y * 8 + z, xh * 2 + c)

    def column(self, step):
        return self.at(z=(self.z + step + 8) % 8)

    def row(self, step):
        return self.at(y=(self.y + step + 4) % 4)

    def diagonal(self, step):
        s = (self.s + step + 8) % 8
        return self.at(
            xl=s // 4, y=jnp.where(s < 4, s, 7 - s), z=(self.z + step + 8) % 8
        )

    def line(self, step):
        x = (self.xh * 2 + self.xl + step + 4) % 4
        return self.at(xh=x // 2, xl=x % 2)

    def other_core(self):
        return self.at(c=1 - self.c)

    def twin(self, other=False):
        return self.at(xh=1 - self.xh, c=1 - self.c if other else self.c)


def remote(src, dst, send, recv, device):
    return pltpu.make_async_remote_copy(
        src_ref=src,
        dst_ref=dst,
        send_sem=send,
        recv_sem=recv,
        device_id=device,
        device_id_type=MESH,
    )


def slot(n, offset):
    return OFFSETS[n].index(n // 2 if offset == -(n // 2) else offset)


class RingGather:
    def __init__(self, n, neighbour, far, own, view, send, recv):
        self.n, self.neighbour, self.far, self.own = n, neighbour, far, own
        self.view, self.send, self.recv = view, send, recv

    def reach(self, direction):
        return self.n // 2 if direction == self.far else self.n // 2 - 1

    def copy(self, direction, step):
        d = 0 if direction == self.far else 1
        src = self.own if step == 1 else self.view(slot(self.n, -direction * (step - 1)))
        return remote(
            src,
            self.view(slot(self.n, -direction * step)),
            self.send.at[d, step - 1],
            self.recv.at[d, step - 1],
            self.neighbour(direction),
        )

    def start(self):
        for direction in (self.far, -self.far):
            self.copy(direction, 1).start()

    def stage(self, step, arrived=None):
        for direction in (self.far, -self.far):
            if step <= self.reach(direction):
                self.copy(direction, step).wait_recv()
                if step < self.reach(direction):
                    self.copy(direction, step + 1).start()
                if arrived is not None:
                    arrived(slot(self.n, -direction * step))

    def finish(self):
        for direction in (self.far, -self.far):
            for step in range(1, self.reach(direction) + 1):
                self.copy(direction, step).wait_send()


class Parcel:
    def __init__(self, out, out_scale, into, into_scale, send, recv, device):
        self.out, self.out_scale = out, out_scale
        self.into, self.into_scale = into, into_scale
        self.data = remote(out, into, send.at[0], recv.at[0], device)
        self.scale = remote(out_scale, into_scale, send.at[1], recv.at[1], device)

    def pack(self, value):
        top = jnp.max(jnp.abs(value), axis=0, keepdims=True)
        top = jnp.maximum(jnp.max(top, axis=1, keepdims=True), 1e-30)
        self.out[...] = (
            jnp.round(value * (32767.0 / top)).astype(jnp.int32).astype(jnp.int16)
        )
        self.out_scale[...] = jnp.broadcast_to(top * (1 / 32767.0), (8, 128))

    def go(self):
        self.data.start()
        self.scale.start()

    def start(self, value):
        self.pack(value)
        self.go()

    def arrive(self):
        self.data.wait_recv()
        self.scale.wait_recv()

    def take(self):
        self.arrive()
        return self.into[...].astype(jnp.int32).astype(jnp.float32) * self.into_scale[0:1, 0:1]

    def sent(self):
        self.data.wait_send()
        self.scale.wait_send()


class RingReduce:
    def __init__(self, n, neighbour, far, part, box):
        self.n, self.neighbour, self.far, self.part, self.box = n, neighbour, far, part, box

    def steps(self, direction):
        return self.n // 2 if direction == self.far else self.n // 2 - 1

    def parcel(self, direction, step):
        out, out_scale, into, into_scale, send, recv = self.box
        i = step - 1 if direction == self.far else self.n // 2 + step - 1
        return Parcel(
            out.at[i], out_scale.at[i], into.at[i], into_scale.at[i],
            send.at[i], recv.at[i], self.neighbour(direction),
        )

    def step(self, direction, step):
        if step > self.steps(direction):
            return
        value = self.part(slot(self.n, direction * (self.steps(direction) + 1 - step)))
        if step > 1:
            value = value + self.parcel(direction, step - 1).take()
        self.parcel(direction, step).start(value)

    def both(self, step):
        self.step(self.far, step)
        self.step(-self.far, step)

    def last(self):
        value = self.part(slot(self.n, 0))
        for direction in (self.far, -self.far):
            value = value + self.parcel(direction, self.steps(direction)).take()
        return value

    def finish(self):
        for direction in (self.far, -self.far):
            for step in range(1, self.steps(direction) + 1):
                self.parcel(direction, step).sent()


def greet(at, meanwhile):
    barrier = pltpu.get_barrier_semaphore()
    others = [at.column(-1), at.column(1), at.diagonal(-1), at.diagonal(1), at.row(-1), at.row(1)]
    others += [at.line(-1), at.line(1), at.other_core(), at.twin(), at.twin(True)]
    for device in others:
        pl.semaphore_signal(barrier, inc=1, device_id=device, device_id_type=MESH)
    meanwhile()
    pl.semaphore_wait(barrier, len(others))


def coefficients(rows, cols, row_ids, col_ids, scale, bias):
    logits = lax.dot_general(
        rows, cols, (((1,), (1,)), ((), ())), preferred_element_type=jnp.float32
    )
    power = jnp.minimum(logits * (scale * -LOG2E) - bias * LOG2E, 126.0)
    sigmoid = 1.0 / (1.0 + jnp.exp2(power))
    label = jnp.where(row_ids == col_ids, 1.0, 0.0)
    return (sigmoid - label).astype(jnp.bfloat16)


def product(coef, rows):
    return jnp.dot(coef, rows, preferred_element_type=jnp.float32)


def product_t(coef, rows):
    return lax.dot_general(
        coef, rows, (((0,), (0,)), ((), ())), preferred_element_type=jnp.float32
    )


def kernel(
    scale, bias, all_ids, a_own, b_own, c_own, a_out, b_out, c_out, a_unit, b_unit, c_unit, ids, ids_t,
    a, b, c, ga, gb, gc, coef_ab, coef_ca, coef_cb,
    a_near, a_box, a_box_scale, b_box, b_box_scale, c_box, c_box_scale, y_box, y_box_scale, sums,
    ga_send, ga_recv, gb_send, gb_recv, gc_send, gc_recv, gt_send, gt_recv, gx_send, gx_recv, own_sem,
    ra_send, ra_recv, rb_send, rb_recv, rc_send, rc_recv, ry_send, ry_recv, rt_send, rt_recv, re_send, re_recv,
):
    at = Place()

    def span(start, size):
        return pl.ds(pl.multiple_of(start, 16), size)

    k = (at.c + at.xh) % 2
    my_b, my_c, my_a = span(at.c * HALF, HALF), span(k * HALF, HALF), span(at.xh * HALF, HALF)
    my_quarter = span(at.xh * HALF + at.c * QUARTER, QUARTER)

    def a_quarter(i, core):
        return a.at[span(i * HALF + core * QUARTER, QUARTER)]

    def piece(ref, i):
        return ref.at[i * HALF : (i + 1) * HALF]

    def quarter(ref, i, part):
        return ref.at[span(i * HALF + part * QUARTER, QUARTER)]

    def c_gather(q):
        own = c_own.at[span(k * HALF + q * QUARTER, QUARTER)]
        return RingGather(8, at.column, 1, own, lambda i: quarter(c, i, q), gc_send.at[q], gc_recv.at[q])

    def b_gather(q):
        return RingGather(4, at.row, 1 - 2 * q, b_share(q), lambda i: quarter(b, i, q), gb_send.at[q], gb_recv.at[q])

    def b_share(q):
        return b_own.at[span(at.c * HALF + q * QUARTER, QUARTER)]

    ring_c = [c_gather(q) for q in range(2)]
    ring_b = [b_gather(q) for q in range(2)]
    ring_a = RingGather(8, at.diagonal, -1, a_own.at[my_quarter], lambda i: a_quarter(i, at.c), ga_send, ga_recv)
    own = [
        pltpu.make_async_copy(a_own.at[my_a], piece(a, 7), own_sem.at[0]),
        pltpu.make_async_copy(b_own.at[my_b], piece(b, 3), own_sem.at[1]),
        pltpu.make_async_copy(c_own.at[my_c], piece(c, 7), own_sem.at[2]),
    ]

    def pass_over(i, core):
        view = a_quarter(i, core)
        return remote(view, view, gt_send.at[i], gt_recv.at[i], at.other_core())

    def over_x(i, q):
        src = b_share(q) if i == 3 else quarter(b, i, q)
        return remote(src, quarter(b, 4 + i, q), gx_send.at[q, i], gx_recv.at[q, i], at.line(1 - 2 * q))

    done = set()

    def once(key, wait):
        if key not in done:
            done.add(key)
            wait()

    def to_other(i):
        pass_over(i, at.c).start()

    def gather_a(step):
        ring_a.stage(step, to_other)

    def gather_b(step):
        for q in range(2):
            ring_b[q].stage(step, lambda i: over_x(i, q).start())

    def b_start():
        for q in range(2):
            ring_b[q].start()

    def x_start():
        for q in range(2):
            over_x(3, q).start()

    def a_here(*groups):
        once("own", lambda: [copy.wait() for copy in own])
        for i in (i for g in groups or range(4) for i in (2 * g, 2 * g + 1)):
            if i < 7:
                once(("a", i), lambda: pass_over(i, 1 - at.c).wait_recv())

    def b_here():
        once("own", lambda: [copy.wait() for copy in own])
        for i in range(4):
            for q in range(2):
                once(("b", i, q), lambda: over_x(i, q).wait_recv())

    def c_here(g):
        once("own", lambda: [copy.wait() for copy in own])

    def ab_rows(g):
        a_here(g)
        b_here()
        rows = pl.ds(g * ROWS, ROWS)
        tile = coefficients(a[rows, :], b[...], ids_t[rows, 0:1], ids[1:2, 0:BLOCK], scale[0], bias[0])
        coef_ab[rows, :] = tile
        ga[rows, :] = scale[0] * product(tile, b[...])

    def cb_rows(g):
        b_here()
        c_here(g)
        rows = pl.ds(g * ROWS, ROWS)
        tile = coefficients(c[rows, :], b[...], ids_t[rows, 2:3], ids[1:2, 0:BLOCK], scale[2], bias[2])
        coef_cb[rows, :] = tile
        gc[rows, :] = scale[2] * product(tile, b[...])

    def ca_rows(g):
        a_here()
        c_here(g)
        rows = pl.ds(g * ROWS, ROWS)
        tile = coefficients(c[rows, :], a[...], ids_t[rows, 2:3], ids[0:1, 0:BLOCK], scale[1], bias[1])
        coef_ca[rows, :] = tile
        gc[rows, :] = gc[rows, :] + scale[1] * product(tile, a[...])

    def a_cols(i):
        cols = pl.ds(i * TILE, TILE)
        ga[cols, :] = ga[cols, :] + scale[1] * product_t(coef_ca[:, cols], c[...])

    def b_cols(i):
        cols = pl.ds(i * TILE, TILE)
        gb[cols, :] = scale[0] * product_t(coef_ab[:, cols], a[...]) + scale[2] * product_t(coef_cb[:, cols], c[...])

    def a_part(i):
        once(("near", i), lambda: near(i, 1 - at.c).wait_recv())
        return ga[pl.ds(pl.multiple_of(i * HALF + at.c * QUARTER, 8), QUARTER), :] + a_near[i]

    reduce_a = RingReduce(
        8, at.diagonal, -1, a_part,
        (a_box.at[0], a_box_scale.at[0], a_box.at[1], a_box_scale.at[1], ra_send, ra_recv),
    )

    def c_ring(q):
        def part(i):
            return gc[i * HALF + q * QUARTER : i * HALF + (q + 1) * QUARTER, :]

        return RingReduce(
            8, at.column, 1, part,
            (c_box.at[0, q], c_box_scale.at[0, q], c_box.at[1, q], c_box_scale.at[1, q], rc_send.at[q], rc_recv.at[q]),
        )

    reduce_c = [c_ring(q) for q in range(2)]
    def x_ring(h):
        next_part = (at.xh + at.xl) % 2
        places = ((0, 1 - at.xh), (1, next_part), (1, 1 - next_part), (0, at.xh))

        def part(i):
            r, quarter_of = places[i]
            return jnp.concatenate(
                [gb[pl.ds(pl.multiple_of((4 * r + 2 * h + j) * HALF + quarter_of * QUARTER, 8), QUARTER), :] for j in range(2)]
            )

        return RingReduce(
            4, at.line, 1 - 2 * h, part,
            (b_box.at[0, h], b_box_scale.at[0, h], b_box.at[1, h], b_box_scale.at[1, h], rb_send.at[h], rb_recv.at[h]),
        )

    reduce_x = [x_ring(h) for h in range(2)]
    reduce_y = RingReduce(
        4, at.row, 1, lambda i: sums[i // 2, i % 2 * QUARTER : (i % 2 + 1) * QUARTER, :],
        (y_box.at[0], y_box_scale.at[0], y_box.at[1], y_box_scale.at[1], ry_send, ry_recv),
    )

    def near(i, core):
        return remote(
            ga.at[pl.ds(pl.multiple_of(i * HALF + core * QUARTER, 8), QUARTER)], a_near.at[i],
            rt_send.at[i], rt_recv.at[i], at.other_core(),
        )

    def rows_of(half, part):
        return span(half * HALF + part * QUARTER, QUARTER)

    def ready(out, unit, half, part, i, device):
        rows, number = out.at[rows_of(half, part)], unit.at[2 * half + part]
        return Parcel(rows, number, rows, number, re_send.at[i], re_recv.at[i], device)

    def to_twin(i):
        if i < 2:
            return ready(c_out.at[at.xh], c_unit.at[at.xh], k, i, i, at.twin(True))
        if i == 2:
            return ready(b_out, b_unit, at.c, at.xh, i, at.twin())
        return ready(a_out, a_unit, at.xh, at.c, i, at.twin())

    def from_twin(i):
        if i < 2:
            return ready(c_out.at[1 - at.xh], c_unit.at[1 - at.xh], k, i, i, at.twin(True))
        if i == 2:
            return ready(b_out, b_unit, at.c, 1 - at.xh, i, at.twin())
        return ready(a_out, a_unit, 1 - at.xh, at.c, i, at.twin())

    def to_core(i, other):
        chip = 1 - at.xh if other else at.xh
        j = 4 + 2 * i + other
        if i < 2:
            return ready(c_out.at[chip], c_unit.at[chip], k, i, j, at.other_core())
        if i == 2:
            return ready(b_out, b_unit, at.c, chip, j, at.other_core())
        return ready(a_out, a_unit, chip, at.c, j, at.other_core())

    def from_core(i, other):
        chip = 1 - at.xh if other else at.xh
        j = 4 + 2 * i + other
        if i < 2:
            return ready(c_out.at[chip], c_unit.at[chip], 1 - k, i, j, at.other_core())
        if i == 2:
            return ready(b_out, b_unit, 1 - at.c, chip, j, at.other_core())
        return ready(a_out, a_unit, chip, 1 - at.c, j, at.other_core())

    def mine_done(i, value):
        to_twin(i).start(value)
        to_core(i, 0).go()

    def other_done(i):
        from_twin(i).arrive()
        to_core(i, 1).go()

    def near_go(i):
        for j in ((0, 1), (2, 3, 4), (5, 6, 7))[i]:
            near(j, 1 - at.c).start()

    def b_last(r):
        sums[r] = reduce_x[r].last()

    steps = {
        "sA": ring_a.start,
        "sC": ring_c[0].start,
        "sD": ring_c[1].start,
        "sP": b_start,
        "sX": x_start,
        "P1": lambda: gather_b(1),
        "P2": lambda: gather_b(2),
        "La": lambda: mine_done(3, reduce_a.last()),
        "Ly": lambda: mine_done(2, reduce_y.last()),
        "Oa": lambda: other_done(3),
        "Ob": lambda: other_done(2),
    }
    for i in range(1, 5):
        steps[f"A{i}"] = lambda i=i: gather_a(i)
        steps[f"C{i}"] = lambda i=i: ring_c[0].stage(i)
        steps[f"D{i}"] = lambda i=i: ring_c[1].stage(i)
    for i in range(4):
        steps[f"ab{i}"] = lambda i=i: ab_rows(i)
        steps[f"cb{i}"] = lambda i=i: cb_rows(i)
        steps[f"ca{i}"] = lambda i=i: ca_rows(i)
    for i in range(3):
        steps[f"ac{i}"] = lambda i=i: a_cols(i)
        steps[f"bc{i}"] = lambda i=i: b_cols(i)
        steps[f"ns{i}"] = lambda i=i: near_go(i)
    for q in range(2):
        steps[f"Lx{q}"] = lambda q=q: b_last(q)
        steps[f"Lc{q}"] = lambda q=q: mine_done(q, reduce_c[q].last())
        steps[f"Sc{q}"] = lambda q=q: other_done(q)
    for name, ring in (("a", reduce_a), ("x0", reduce_x[0]), ("x1", reduce_x[1]), ("c0", reduce_c[0]), ("c1", reduce_c[1]), ("y", reduce_y)):
        for way, direction in (("f", ring.far), ("n", -ring.far)):
            for i in range(1, ring.steps(direction) + 1):
                steps[f"{name}{way}{i}"] = lambda ring=ring, d=direction, i=i: ring.step(d, i)

    def shards_of(which):
        if which == 0:
            return [at.diagonal(o)[0] for o in OFFSETS[8]], at.xh
        if which == 1:
            return [at.at(xl=xl, y=(at.y + o + 4) % 4)[0] for xl in (at.xl, 1 - at.xl) for o in OFFSETS[4]], at.c
        return [at.column(o)[0] for o in OFFSETS[8]], k

    def lay_out_ids():
        ids[...] = jnp.zeros_like(ids)
        lane = lax.broadcasted_iota(jnp.int32, (3, 256), 1)
        row = lax.broadcasted_iota(jnp.int32, (3, 256), 0)
        for which in range(3):
            shards, half = shards_of(which)
            for i, shard in enumerate(shards):
                base = shard * ROWS + half * HALF
                start = base // 128 * 128 - base // (TOKENS - HALF) * 128
                window = all_ids[:, pl.ds(pl.multiple_of(start, 128), 256)]
                first = i * HALF % 128
                moved = pltpu.roll(window, (first - base + start + 256) % 256, 1)
                here = (row == which) & (lane >= first) & (lane < first + HALF)
                place = (slice(0, 3), slice(i * HALF - first, i * HALF - first + 256))
                ids[place] = jnp.where(here, moved, ids[place])
        ids_t[...] = jnp.transpose(ids[:, 0:BLOCK])

    for copy in own:
        copy.start()
    greet(at, lay_out_ids)
    for name in ORDER:
        steps[name]()

    for ring in (ring_a, *ring_c, *ring_b, reduce_a, reduce_y, *reduce_c, *reduce_x):
        ring.finish()
    for i in range(7):
        pass_over(i, at.c).wait_send()
    for i in range(4):
        for q in range(2):
            over_x(i, q).wait_send()
    for i in range(8):
        near(i, 1 - at.c).wait_send()
    for i in range(4):
        to_twin(i).sent()
        for other in range(2):
            to_core(i, other).sent()
            from_core(i, other).arrive()


def gradients(scale, bias, ids, a, b, c):
    vmem = pl.BlockSpec(memory_space=pltpu.VMEM)
    smem = pl.BlockSpec(memory_space=pltpu.SMEM)
    hbm = pl.BlockSpec(memory_space=pl.ANY)
    dma = pltpu.SemaphoreType.DMA
    f32, bf16, i16 = jnp.float32, jnp.bfloat16, jnp.int16
    m = pltpu.VMEM
    shape = jax.ShapeDtypeStruct
    a, b, c, a_unit, b_unit, c_unit = pl.pallas_call(
        kernel,
        out_shape=(
            shape((ROWS, WIDTH), i16), shape((ROWS, WIDTH), i16), shape((2, ROWS, WIDTH), i16),
            shape((4, 8, 128), f32), shape((4, 8, 128), f32), shape((2, 4, 8, 128), f32),
        ),
        in_specs=[smem, smem, vmem] + [hbm] * 3,
        out_specs=(vmem,) * 6,
        scratch_shapes=[
            m((8, 896), jnp.int32), m((BLOCK, 8), jnp.int32),
            m((BLOCK, WIDTH), bf16), m((BLOCK, WIDTH), bf16), m((BLOCK, WIDTH), bf16),
            m((BLOCK, WIDTH), f32), m((BLOCK, WIDTH), f32), m((BLOCK, WIDTH), f32),
            m((BLOCK, BLOCK), bf16), m((BLOCK, BLOCK), bf16), m((BLOCK, BLOCK), bf16),
            m((8, QUARTER, WIDTH), f32),
            m((2, 7, QUARTER, WIDTH), i16), m((2, 7, 8, 128), f32),
            m((2, 2, 3, HALF, WIDTH), i16), m((2, 2, 3, 8, 128), f32),
            m((2, 2, 7, QUARTER, WIDTH), i16), m((2, 2, 7, 8, 128), f32),
            m((2, 3, QUARTER, WIDTH), i16), m((2, 3, 8, 128), f32),
            m((2, HALF, WIDTH), f32),
            dma((2, 4)), dma((2, 4)), dma((2, 2, 2)), dma((2, 2, 2)), dma((2, 2, 4)), dma((2, 2, 4)),
            dma((7,)), dma((7,)), dma((2, 4)), dma((2, 4)), dma((3,)),
            dma((7, 2)), dma((7, 2)), dma((2, 3, 2)), dma((2, 3, 2)), dma((2, 7, 2)), dma((2, 7, 2)), dma((3, 2)), dma((3, 2)),
            dma((8,)), dma((8,)), dma((12, 2)), dma((12, 2)),
        ],
        compiler_params=pltpu.CompilerParams(
            collective_id=0, has_side_effects=True, vmem_limit_bytes=56 << 20
        ),
    )(scale, bias, ids, a, b, c)
    return decode(a, b, c, a_unit, b_unit, c_unit)


def decode_kernel(a, b, c, a_unit, b_unit, c_unit, a_out, b_out, c_out):
    def value(code, unit):
        return code.astype(jnp.int32).astype(jnp.float32) * unit[0:1, 0:1]

    for i in range(4):
        rows = pl.ds(i * QUARTER, QUARTER)
        a_out[rows, :] = value(a[rows, :], a_unit[i])
        b_out[rows, :] = value(b[rows, :], b_unit[i])
        c_out[rows, :] = value(c[0, rows, :], c_unit[0, i]) + value(c[1, rows, :], c_unit[1, i])


def decode(a, b, c, a_unit, b_unit, c_unit):
    vmem = pl.BlockSpec(memory_space=pltpu.VMEM)
    out = jax.ShapeDtypeStruct((ROWS, WIDTH), jnp.float32)
    return pl.pallas_call(
        decode_kernel,
        out_shape=(out, out, out),
        in_specs=[vmem] * 6,
        out_specs=(vmem, vmem, vmem),
    )(a, b, c, a_unit, b_unit, c_unit)


def body(event, lidar, frame, sample_ids, logit_scale, logit_bias):
    return gradients(logit_scale, logit_bias, sample_ids, event, lidar, frame)


def solution(mesh):
    placed = (P("dp", None), P("dp", None), P("dp", None), P(), P(), P())
    return jax.shard_map(
        body,
        mesh=mesh,
        in_specs=placed,
        out_specs=(P("dp", None), P("dp", None), P("dp", None)),
        check_vma=False,
    )
```

```python
import math

import jax
import jax.numpy as jnp
from jax import lax
from jax.experimental import pallas as pl
from jax.experimental.pallas import tpu as pltpu
from jax.sharding import PartitionSpec as P

MESH = pl.DeviceIdType.MESH
ROWS = 192
HALF = 96
QUARTER = 48
WIDTH = 1024
BLOCK = 768
TOKENS = 12288
TILE = 256
LOG2E = math.log2(math.e)
OFFSETS = {8: (4, 3, -3, 2, -2, 1, -1, 0), 4: (2, 1, -1, 0)}

ORDER = (
    "sC", "sP", "sX", "sA", "sD", "ids", "P1", "D1", "C1", "P2", "A1", "C2", "A2", "ab2", "D2", "ab3",
    "cb3", "A3", "C3", "cb2", "D3", "cb1", "ab1", "A4", "C4", "ab0", "ca1", "D4", "cb0", "ca0", "c1f1",
    "c0n1", "bc0", "bc1", "c0f1", "x0f1", "x1f1", "bc2", "c1n1", "ca2", "c1f2", "ca3", "c0n2", "x1n1",
    "ac0", "ns0", "x0n1", "c0f2", "af1", "ac2", "c1f3", "x1f2", "x0f2", "an1", "c1n2", "ac1", "ns1",
    "c0f3", "af2", "c1n3", "ns2", "c1f4", "Lx0", "yf1", "Lx1", "yn1", "c0f4", "c0n3", "Lc1", "an2",
    "af3", "yf2", "Lc0", "af4", "an3", "Ly", "La", "Sc1", "Sc0", "Ob", "Oa",
)


class Place:
    def __init__(self):
        dp, group = lax.axis_index("dp"), lax.axis_index("group")
        self.xl, self.y, self.z = dp // 32, (dp // 8) % 4, dp % 8
        self.xh, self.c = group // 2, group % 2
        self.s = jnp.where(self.xl == 0, self.y, 7 - self.y)

    def at(self, xh=None, xl=None, y=None, z=None, c=None):
        xh, xl = self.xh if xh is None else xh, self.xl if xl is None else xl
        y, z = self.y if y is None else y, self.z if z is None else z
        c = self.c if c is None else c
        return (xl * 32 + y * 8 + z, xh * 2 + c)

    def column(self, step):
        return self.at(z=(self.z + step + 8) % 8)

    def row(self, step):
        return self.at(y=(self.y + step + 4) % 4)

    def diagonal(self, step):
        s = (self.s + step + 8) % 8
        return self.at(
            xl=s // 4, y=jnp.where(s < 4, s, 7 - s), z=(self.z + step + 8) % 8
        )

    def line(self, step):
        x = (self.xh * 2 + self.xl + step + 4) % 4
        return self.at(xh=x // 2, xl=x % 2)

    def other_core(self):
        return self.at(c=1 - self.c)

    def twin(self, other=False):
        return self.at(xh=1 - self.xh, c=1 - self.c if other else self.c)


def remote(src, dst, send, recv, device):
    return pltpu.make_async_remote_copy(
        src_ref=src,
        dst_ref=dst,
        send_sem=send,
        recv_sem=recv,
        device_id=device,
        device_id_type=MESH,
    )


def slot(n, offset):
    return OFFSETS[n].index(n // 2 if offset == -(n // 2) else offset)


class RingGather:
    def __init__(self, n, neighbour, far, own, view, send, recv):
        self.n, self.neighbour, self.far, self.own = n, neighbour, far, own
        self.view, self.send, self.recv = view, send, recv

    def reach(self, direction):
        return self.n // 2 if direction == self.far else self.n // 2 - 1

    def copy(self, direction, step):
        d = 0 if direction == self.far else 1
        src = self.own if step == 1 else self.view(slot(self.n, -direction * (step - 1)))
        return remote(
            src,
            self.view(slot(self.n, -direction * step)),
            self.send.at[d, step - 1],
            self.recv.at[d, step - 1],
            self.neighbour(direction),
        )

    def start(self):
        for direction in (self.far, -self.far):
            self.copy(direction, 1).start()

    def stage(self, step, arrived=None):
        for direction in (self.far, -self.far):
            if step <= self.reach(direction):
                self.copy(direction, step).wait_recv()
                if step < self.reach(direction):
                    self.copy(direction, step + 1).start()
                if arrived is not None:
                    arrived(slot(self.n, -direction * step))

    def finish(self):
        for direction in (self.far, -self.far):
            for step in range(1, self.reach(direction) + 1):
                self.copy(direction, step).wait_send()


class Parcel:
    def __init__(self, out, out_scale, into, into_scale, send, recv, device):
        self.out, self.out_scale = out, out_scale
        self.into, self.into_scale = into, into_scale
        self.data = remote(out, into, send.at[0], recv.at[0], device)
        self.scale = remote(out_scale, into_scale, send.at[1], recv.at[1], device)

    def pack(self, value):
        top = jnp.max(jnp.abs(value), axis=0, keepdims=True)
        top = jnp.maximum(jnp.max(top, axis=1, keepdims=True), 1e-30)
        self.out[...] = (
            jnp.round(value * (32767.0 / top)).astype(jnp.int32).astype(jnp.int16)
        )
        self.out_scale[...] = jnp.broadcast_to(top * (1 / 32767.0), (8, 128))

    def go(self):
        self.data.start()
        self.scale.start()

    def start(self, value):
        self.pack(value)
        self.go()

    def arrive(self):
        self.data.wait_recv()
        self.scale.wait_recv()

    def take(self):
        self.arrive()
        return self.into[...].astype(jnp.int32).astype(jnp.float32) * self.into_scale[0:1, 0:1]

    def sent(self):
        self.data.wait_send()
        self.scale.wait_send()


class RingReduce:
    def __init__(self, n, neighbour, far, part, box):
        self.n, self.neighbour, self.far, self.part, self.box = n, neighbour, far, part, box

    def steps(self, direction):
        return self.n // 2 if direction == self.far else self.n // 2 - 1

    def parcel(self, direction, step):
        out, out_scale, into, into_scale, send, recv = self.box
        i = step - 1 if direction == self.far else self.n // 2 + step - 1
        return Parcel(
            out.at[i], out_scale.at[i], into.at[i], into_scale.at[i],
            send.at[i], recv.at[i], self.neighbour(direction),
        )

    def step(self, direction, step):
        if step > self.steps(direction):
            return
        value = self.part(slot(self.n, direction * (self.steps(direction) + 1 - step)))
        if step > 1:
            value = value + self.parcel(direction, step - 1).take()
        self.parcel(direction, step).start(value)

    def both(self, step):
        self.step(self.far, step)
        self.step(-self.far, step)

    def last(self):
        value = self.part(slot(self.n, 0))
        for direction in (self.far, -self.far):
            value = value + self.parcel(direction, self.steps(direction)).take()
        return value

    def finish(self):
        for direction in (self.far, -self.far):
            for step in range(1, self.steps(direction) + 1):
                self.parcel(direction, step).sent()


def greet(at):
    barrier = pltpu.get_barrier_semaphore()
    others = [at.column(-1), at.column(1), at.diagonal(-1), at.diagonal(1), at.row(-1), at.row(1)]
    others += [at.line(-1), at.line(1), at.other_core(), at.twin(), at.twin(True)]
    for device in others:
        pl.semaphore_signal(barrier, inc=1, device_id=device, device_id_type=MESH)
    pl.semaphore_wait(barrier, len(others))


def coefficients(rows, cols, row_ids, col_ids, scale, bias):
    logits = lax.dot_general(
        rows, cols, (((1,), (1,)), ((), ())), preferred_element_type=jnp.float32
    )
    power = jnp.minimum(logits * (scale * -LOG2E) - bias * LOG2E, 126.0)
    sigmoid = 1.0 / (1.0 + jnp.exp2(power))
    label = jnp.where(row_ids == col_ids, 1.0, 0.0)
    return (sigmoid - label).astype(jnp.bfloat16)


def product(coef, rows):
    return jnp.dot(coef, rows, preferred_element_type=jnp.float32)


def product_t(coef, rows):
    return lax.dot_general(
        coef, rows, (((0,), (0,)), ((), ())), preferred_element_type=jnp.float32
    )


def kernel(
    scale, bias, ids_in, a_own, b_own, c_own, a_out, b_out, c_out, a_unit, b_unit, c_unit, all_ids, ids, ids_t,
    a, b, c, ga, gb, gc, coef_ab, coef_ca, coef_cb,
    a_near, a_box, a_box_scale, b_box, b_box_scale, c_box, c_box_scale, y_box, y_box_scale, sums,
    ga_send, ga_recv, gb_send, gb_recv, gc_send, gc_recv, gt_send, gt_recv, gx_send, gx_recv, own_sem,
    ra_send, ra_recv, rb_send, rb_recv, rc_send, rc_recv, ry_send, ry_recv, rt_send, rt_recv, re_send, re_recv,
):
    at = Place()

    def span(start, size):
        return pl.ds(pl.multiple_of(start, 16), size)

    k = (at.c + at.xh) % 2
    my_b, my_c, my_a = span(at.c * HALF, HALF), span(k * HALF, HALF), span(at.xh * HALF, HALF)
    my_quarter = span(at.xh * HALF + at.c * QUARTER, QUARTER)

    def a_quarter(i, core):
        return a.at[span(i * HALF + core * QUARTER, QUARTER)]

    def piece(ref, i):
        return ref.at[i * HALF : (i + 1) * HALF]

    def quarter(ref, i, part):
        return ref.at[span(i * HALF + part * QUARTER, QUARTER)]

    def c_gather(q):
        own = c_own.at[span(k * HALF + q * QUARTER, QUARTER)]
        return RingGather(8, at.column, 1, own, lambda i: quarter(c, i, q), gc_send.at[q], gc_recv.at[q])

    def b_gather(q):
        return RingGather(4, at.row, 1 - 2 * q, b_share(q), lambda i: quarter(b, i, q), gb_send.at[q], gb_recv.at[q])

    def b_share(q):
        return b_own.at[span(at.c * HALF + q * QUARTER, QUARTER)]

    ring_c = [c_gather(q) for q in range(2)]
    ring_b = [b_gather(q) for q in range(2)]
    ring_a = RingGather(8, at.diagonal, -1, a_own.at[my_quarter], lambda i: a_quarter(i, at.c), ga_send, ga_recv)
    own = [
        pltpu.make_async_copy(a_own.at[my_a], piece(a, 7), own_sem.at[0]),
        pltpu.make_async_copy(b_own.at[my_b], piece(b, 3), own_sem.at[1]),
        pltpu.make_async_copy(c_own.at[my_c], piece(c, 7), own_sem.at[2]),
    ]

    def pass_over(i, core):
        view = a_quarter(i, core)
        return remote(view, view, gt_send.at[i], gt_recv.at[i], at.other_core())

    def over_x(i, q):
        src = b_share(q) if i == 3 else quarter(b, i, q)
        return remote(src, quarter(b, 4 + i, q), gx_send.at[q, i], gx_recv.at[q, i], at.line(1 - 2 * q))

    done = set()

    def once(key, wait):
        if key not in done:
            done.add(key)
            wait()

    def to_other(i):
        pass_over(i, at.c).start()

    def gather_a(step):
        ring_a.stage(step, to_other)

    def gather_b(step):
        for q in range(2):
            ring_b[q].stage(step, lambda i: over_x(i, q).start())

    def b_start():
        for q in range(2):
            ring_b[q].start()

    def x_start():
        for q in range(2):
            over_x(3, q).start()

    def a_here(*groups):
        once("own", lambda: [copy.wait() for copy in own])
        for i in (i for g in groups or range(4) for i in (2 * g, 2 * g + 1)):
            if i < 7:
                once(("a", i), lambda: pass_over(i, 1 - at.c).wait_recv())

    def b_here():
        once("own", lambda: [copy.wait() for copy in own])
        for i in range(4):
            for q in range(2):
                once(("b", i, q), lambda: over_x(i, q).wait_recv())

    def c_here(g):
        once("own", lambda: [copy.wait() for copy in own])

    def ab_rows(g):
        a_here(g)
        b_here()
        rows = pl.ds(g * ROWS, ROWS)
        tile = coefficients(a[rows, :], b[...], ids_t[rows, 0:1], ids[1:2, 0:BLOCK], scale[0], bias[0])
        coef_ab[rows, :] = tile
        ga[rows, :] = scale[0] * product(tile, b[...])

    def cb_rows(g):
        b_here()
        c_here(g)
        rows = pl.ds(g * ROWS, ROWS)
        tile = coefficients(c[rows, :], b[...], ids_t[rows, 2:3], ids[1:2, 0:BLOCK], scale[2], bias[2])
        coef_cb[rows, :] = tile
        gc[rows, :] = scale[2] * product(tile, b[...])

    def ca_rows(g):
        a_here()
        c_here(g)
        rows = pl.ds(g * ROWS, ROWS)
        tile = coefficients(c[rows, :], a[...], ids_t[rows, 2:3], ids[0:1, 0:BLOCK], scale[1], bias[1])
        coef_ca[rows, :] = tile
        gc[rows, :] = gc[rows, :] + scale[1] * product(tile, a[...])

    def a_cols(i):
        cols = pl.ds(i * TILE, TILE)
        ga[cols, :] = ga[cols, :] + scale[1] * product_t(coef_ca[:, cols], c[...])

    def b_cols(i):
        cols = pl.ds(i * TILE, TILE)
        gb[cols, :] = scale[0] * product_t(coef_ab[:, cols], a[...]) + scale[2] * product_t(coef_cb[:, cols], c[...])

    def a_part(i):
        once(("near", i), lambda: near(i, 1 - at.c).wait_recv())
        return ga[pl.ds(pl.multiple_of(i * HALF + at.c * QUARTER, 8), QUARTER), :] + a_near[i]

    reduce_a = RingReduce(
        8, at.diagonal, -1, a_part,
        (a_box.at[0], a_box_scale.at[0], a_box.at[1], a_box_scale.at[1], ra_send, ra_recv),
    )

    def c_ring(q):
        def part(i):
            return gc[i * HALF + q * QUARTER : i * HALF + (q + 1) * QUARTER, :]

        return RingReduce(
            8, at.column, 1, part,
            (c_box.at[0, q], c_box_scale.at[0, q], c_box.at[1, q], c_box_scale.at[1, q], rc_send.at[q], rc_recv.at[q]),
        )

    reduce_c = [c_ring(q) for q in range(2)]
    def x_ring(h):
        next_part = (at.xh + at.xl) % 2
        places = ((0, 1 - at.xh), (1, next_part), (1, 1 - next_part), (0, at.xh))

        def part(i):
            r, quarter_of = places[i]
            return jnp.concatenate(
                [gb[pl.ds(pl.multiple_of((4 * r + 2 * h + j) * HALF + quarter_of * QUARTER, 8), QUARTER), :] for j in range(2)]
            )

        return RingReduce(
            4, at.line, 1 - 2 * h, part,
            (b_box.at[0, h], b_box_scale.at[0, h], b_box.at[1, h], b_box_scale.at[1, h], rb_send.at[h], rb_recv.at[h]),
        )

    reduce_x = [x_ring(h) for h in range(2)]
    reduce_y = RingReduce(
        4, at.row, 1, lambda i: sums[i // 2, i % 2 * QUARTER : (i % 2 + 1) * QUARTER, :],
        (y_box.at[0], y_box_scale.at[0], y_box.at[1], y_box_scale.at[1], ry_send, ry_recv),
    )

    def near(i, core):
        return remote(
            ga.at[pl.ds(pl.multiple_of(i * HALF + core * QUARTER, 8), QUARTER)], a_near.at[i],
            rt_send.at[i], rt_recv.at[i], at.other_core(),
        )

    def rows_of(half, part):
        return span(half * HALF + part * QUARTER, QUARTER)

    def ready(out, unit, half, part, i, device):
        rows, number = out.at[rows_of(half, part)], unit.at[2 * half + part]
        return Parcel(rows, number, rows, number, re_send.at[i], re_recv.at[i], device)

    def to_twin(i):
        if i < 2:
            return ready(c_out.at[at.xh], c_unit.at[at.xh], k, i, i, at.twin(True))
        if i == 2:
            return ready(b_out, b_unit, at.c, at.xh, i, at.twin())
        return ready(a_out, a_unit, at.xh, at.c, i, at.twin())

    def from_twin(i):
        if i < 2:
            return ready(c_out.at[1 - at.xh], c_unit.at[1 - at.xh], k, i, i, at.twin(True))
        if i == 2:
            return ready(b_out, b_unit, at.c, 1 - at.xh, i, at.twin())
        return ready(a_out, a_unit, 1 - at.xh, at.c, i, at.twin())

    def to_core(i, other):
        chip = 1 - at.xh if other else at.xh
        j = 4 + 2 * i + other
        if i < 2:
            return ready(c_out.at[chip], c_unit.at[chip], k, i, j, at.other_core())
        if i == 2:
            return ready(b_out, b_unit, at.c, chip, j, at.other_core())
        return ready(a_out, a_unit, chip, at.c, j, at.other_core())

    def from_core(i, other):
        chip = 1 - at.xh if other else at.xh
        j = 4 + 2 * i + other
        if i < 2:
            return ready(c_out.at[chip], c_unit.at[chip], 1 - k, i, j, at.other_core())
        if i == 2:
            return ready(b_out, b_unit, 1 - at.c, chip, j, at.other_core())
        return ready(a_out, a_unit, chip, 1 - at.c, j, at.other_core())

    def mine_done(i, value):
        to_twin(i).start(value)
        to_core(i, 0).go()

    def other_done(i):
        from_twin(i).arrive()
        to_core(i, 1).go()

    def near_go(i):
        for j in ((0, 1), (2, 3, 4), (5, 6, 7))[i]:
            near(j, 1 - at.c).start()

    def b_last(r):
        sums[r] = reduce_x[r].last()

    steps = {
        "sA": ring_a.start,
        "sC": ring_c[0].start,
        "sD": ring_c[1].start,
        "sP": b_start,
        "sX": x_start,
        "P1": lambda: gather_b(1),
        "P2": lambda: gather_b(2),
        "La": lambda: mine_done(3, reduce_a.last()),
        "Ly": lambda: mine_done(2, reduce_y.last()),
        "Oa": lambda: other_done(3),
        "Ob": lambda: other_done(2),
    }
    for i in range(1, 5):
        steps[f"A{i}"] = lambda i=i: gather_a(i)
        steps[f"C{i}"] = lambda i=i: ring_c[0].stage(i)
        steps[f"D{i}"] = lambda i=i: ring_c[1].stage(i)
    for i in range(4):
        steps[f"ab{i}"] = lambda i=i: ab_rows(i)
        steps[f"cb{i}"] = lambda i=i: cb_rows(i)
        steps[f"ca{i}"] = lambda i=i: ca_rows(i)
    for i in range(3):
        steps[f"ac{i}"] = lambda i=i: a_cols(i)
        steps[f"bc{i}"] = lambda i=i: b_cols(i)
        steps[f"ns{i}"] = lambda i=i: near_go(i)
    for q in range(2):
        steps[f"Lx{q}"] = lambda q=q: b_last(q)
        steps[f"Lc{q}"] = lambda q=q: mine_done(q, reduce_c[q].last())
        steps[f"Sc{q}"] = lambda q=q: other_done(q)
    for name, ring in (("a", reduce_a), ("x0", reduce_x[0]), ("x1", reduce_x[1]), ("c0", reduce_c[0]), ("c1", reduce_c[1]), ("y", reduce_y)):
        for way, direction in (("f", ring.far), ("n", -ring.far)):
            for i in range(1, ring.steps(direction) + 1):
                steps[f"{name}{way}{i}"] = lambda ring=ring, d=direction, i=i: ring.step(d, i)

    def shards_of(which):
        if which == 0:
            return [at.diagonal(o)[0] for o in OFFSETS[8]], at.xh
        if which == 1:
            return [at.at(xl=xl, y=(at.y + o + 4) % 4)[0] for xl in (at.xl, 1 - at.xl) for o in OFFSETS[4]], at.c
        return [at.column(o)[0] for o in OFFSETS[8]], k

    def lay_out_ids():
        ids_copy.wait()
        ids[...] = jnp.zeros_like(ids)
        lane = lax.broadcasted_iota(jnp.int32, (3, 256), 1)
        row = lax.broadcasted_iota(jnp.int32, (3, 256), 0)
        for which in range(3):
            shards, half = shards_of(which)
            for i, shard in enumerate(shards):
                base = shard * ROWS + half * HALF
                start = base // 128 * 128 - base // (TOKENS - HALF) * 128
                window = all_ids[:, pl.ds(pl.multiple_of(start, 128), 256)]
                first = i * HALF % 128
                moved = pltpu.roll(window, (first - base + start + 256) % 256, 1)
                here = (row == which) & (lane >= first) & (lane < first + HALF)
                place = (slice(0, 3), slice(i * HALF - first, i * HALF - first + 256))
                ids[place] = jnp.where(here, moved, ids[place])
        ids_t[...] = jnp.transpose(ids[:, 0:BLOCK])

    ids_copy = pltpu.make_async_copy(ids_in, all_ids, own_sem.at[3])
    steps["ids"] = lay_out_ids
    ids_copy.start()
    for copy in own:
        copy.start()
    greet(at)
    for name in ORDER:
        steps[name]()

    for ring in (ring_a, *ring_c, *ring_b, reduce_a, reduce_y, *reduce_c, *reduce_x):
        ring.finish()
    for i in range(7):
        pass_over(i, at.c).wait_send()
    for i in range(4):
        for q in range(2):
            over_x(i, q).wait_send()
    for i in range(8):
        near(i, 1 - at.c).wait_send()
    for i in range(4):
        to_twin(i).sent()
        for other in range(2):
            to_core(i, other).sent()
            from_core(i, other).arrive()


def gradients(scale, bias, ids, a, b, c):
    vmem = pl.BlockSpec(memory_space=pltpu.VMEM)
    smem = pl.BlockSpec(memory_space=pltpu.SMEM)
    hbm = pl.BlockSpec(memory_space=pl.ANY)
    dma = pltpu.SemaphoreType.DMA
    f32, bf16, i16 = jnp.float32, jnp.bfloat16, jnp.int16
    m = pltpu.VMEM
    shape = jax.ShapeDtypeStruct
    a, b, c, a_unit, b_unit, c_unit = pl.pallas_call(
        kernel,
        out_shape=(
            shape((ROWS, WIDTH), i16), shape((ROWS, WIDTH), i16), shape((2, ROWS, WIDTH), i16),
            shape((4, 8, 128), f32), shape((4, 8, 128), f32), shape((2, 4, 8, 128), f32),
        ),
        in_specs=[smem, smem] + [hbm] * 4,
        out_specs=(vmem,) * 6,
        scratch_shapes=[
            m((3, TOKENS), jnp.int32), m((8, 896), jnp.int32), m((BLOCK, 8), jnp.int32),
            m((BLOCK, WIDTH), bf16), m((BLOCK, WIDTH), bf16), m((BLOCK, WIDTH), bf16),
            m((BLOCK, WIDTH), f32), m((BLOCK, WIDTH), f32), m((BLOCK, WIDTH), f32),
            m((BLOCK, BLOCK), bf16), m((BLOCK, BLOCK), bf16), m((BLOCK, BLOCK), bf16),
            m((8, QUARTER, WIDTH), f32),
            m((2, 7, QUARTER, WIDTH), i16), m((2, 7, 8, 128), f32),
            m((2, 2, 3, HALF, WIDTH), i16), m((2, 2, 3, 8, 128), f32),
            m((2, 2, 7, QUARTER, WIDTH), i16), m((2, 2, 7, 8, 128), f32),
            m((2, 3, QUARTER, WIDTH), i16), m((2, 3, 8, 128), f32),
            m((2, HALF, WIDTH), f32),
            dma((2, 4)), dma((2, 4)), dma((2, 2, 2)), dma((2, 2, 2)), dma((2, 2, 4)), dma((2, 2, 4)),
            dma((7,)), dma((7,)), dma((2, 4)), dma((2, 4)), dma((4,)),
            dma((7, 2)), dma((7, 2)), dma((2, 3, 2)), dma((2, 3, 2)), dma((2, 7, 2)), dma((2, 7, 2)), dma((3, 2)), dma((3, 2)),
            dma((8,)), dma((8,)), dma((12, 2)), dma((12, 2)),
        ],
        compiler_params=pltpu.CompilerParams(
            collective_id=0, has_side_effects=True, vmem_limit_bytes=56 << 20
        ),
    )(scale, bias, ids, a, b, c)
    return decode(a, b, c, a_unit, b_unit, c_unit)


def decode_kernel(
    a, b, c, a_unit, b_unit, c_unit, a_out, b_out, c_out, codes, units, values, sems
):
    jobs = ((a, a_unit, 0), (b, b_unit, 1), (c.at[0], c_unit.at[0], 2), (c.at[1], c_unit.at[1], 3))
    reads = [
        (
            pltpu.make_async_copy(code, codes.at[i], sems.at[0, i]),
            pltpu.make_async_copy(unit, units.at[i], sems.at[1, i]),
        )
        for code, unit, i in jobs
    ]
    for pair in reads:
        for copy in pair:
            copy.start()

    def value(i, j):
        code = codes[i, j * QUARTER : (j + 1) * QUARTER, :]
        return code.astype(jnp.int32).astype(jnp.float32) * units[i, j, 0:1, 0:1]

    writes = []
    for n, (terms, out) in enumerate((((0,), a_out), ((1,), b_out), ((2, 3), c_out))):
        for i in terms:
            for copy in reads[i]:
                copy.wait()
        for j in range(4):
            total = value(terms[0], j)
            if len(terms) == 2:
                total = total + value(terms[1], j)
            values[n, j * QUARTER : (j + 1) * QUARTER, :] = total
        writes.append(pltpu.make_async_copy(values.at[n], out, sems.at[2, n]))
        writes[-1].start()
    for copy in writes:
        copy.wait()


def decode(a, b, c, a_unit, b_unit, c_unit):
    hbm = pl.BlockSpec(memory_space=pl.ANY)
    out = jax.ShapeDtypeStruct((ROWS, WIDTH), jnp.float32)
    return pl.pallas_call(
        decode_kernel,
        out_shape=(out, out, out),
        in_specs=[hbm] * 6,
        out_specs=(hbm, hbm, hbm),
        scratch_shapes=[
            pltpu.VMEM((4, ROWS, WIDTH), jnp.int16),
            pltpu.VMEM((4, 4, 8, 128), jnp.float32),
            pltpu.VMEM((3, ROWS, WIDTH), jnp.float32),
            pltpu.SemaphoreType.DMA((3, 4)),
        ],
        compiler_params=pltpu.CompilerParams(vmem_limit_bytes=56 << 20),
    )(a, b, c, a_unit, b_unit, c_unit)


def body(event, lidar, frame, sample_ids, logit_scale, logit_bias):
    return gradients(logit_scale, logit_bias, sample_ids, event, lidar, frame)


def solution(mesh):
    placed = (P("dp", None), P("dp", None), P("dp", None), P(), P(), P())
    return jax.shard_map(
        body,
        mesh=mesh,
        in_specs=placed,
        out_specs=(P("dp", None), P("dp", None), P("dp", None)),
        check_vma=False,
    )
```

```python
import math

import jax
import jax.numpy as jnp
from jax import lax
from jax.experimental import pallas as pl
from jax.experimental.pallas import tpu as pltpu
from jax.sharding import PartitionSpec as P

MESH = pl.DeviceIdType.MESH
ROWS = 192
HALF = 96
QUARTER = 48
WIDTH = 1024
BLOCK = 768
TOKENS = 12288
TILE = 256
LOG2E = math.log2(math.e)
OFFSETS = {8: (4, 3, -3, 2, -2, 1, -1, 0), 4: (2, 1, -1, 0)}

ORDER = (
    "sC", "sP", "sX", "sA", "sD", "ids", "P1", "D1", "C1", "P2", "A1", "C2", "A2", "ab2", "D2", "ab3",
    "cb3", "A3", "C3", "cb2", "D3", "cb1", "ab1", "A4", "C4", "ab0", "ca1", "D4", "cb0", "ca0", "c1f1",
    "c0n1", "bc0", "bc1", "c0f1", "x0f1", "x1f1", "bc2", "c1n1", "ca2", "c1f2", "ca3", "c0n2", "x1n1",
    "ac0", "ns0", "x0n1", "c0f2", "af1", "ac2", "c1f3", "x1f2", "x0f2", "an1", "c1n2", "ac1", "ns1",
    "c0f3", "af2", "c1n3", "ns2", "c1f4", "Lx0", "yf1", "Lx1", "yn1", "c0f4", "c0n3", "Lc1", "an2",
    "af3", "yf2", "Lc0", "af4", "an3", "Ly", "La", "Sc1", "Sc0", "Ob", "Oa",
)


class Place:
    def __init__(self):
        dp, group = lax.axis_index("dp"), lax.axis_index("group")
        self.xl, self.y, self.z = dp // 32, (dp // 8) % 4, dp % 8
        self.xh, self.c = group // 2, group % 2
        self.s = jnp.where(self.xl == 0, self.y, 7 - self.y)

    def at(self, xh=None, xl=None, y=None, z=None, c=None):
        xh, xl = self.xh if xh is None else xh, self.xl if xl is None else xl
        y, z = self.y if y is None else y, self.z if z is None else z
        c = self.c if c is None else c
        return (xl * 32 + y * 8 + z, xh * 2 + c)

    def column(self, step):
        return self.at(z=(self.z + step + 8) % 8)

    def row(self, step):
        return self.at(y=(self.y + step + 4) % 4)

    def diagonal(self, step):
        s = (self.s + step + 8) % 8
        return self.at(
            xl=s // 4, y=jnp.where(s < 4, s, 7 - s), z=(self.z + step + 8) % 8
        )

    def line(self, step):
        x = (self.xh * 2 + self.xl + step + 4) % 4
        return self.at(xh=x // 2, xl=x % 2)

    def other_core(self):
        return self.at(c=1 - self.c)

    def twin(self, other=False):
        return self.at(xh=1 - self.xh, c=1 - self.c if other else self.c)


def remote(src, dst, send, recv, device):
    return pltpu.make_async_remote_copy(
        src_ref=src,
        dst_ref=dst,
        send_sem=send,
        recv_sem=recv,
        device_id=device,
        device_id_type=MESH,
    )


def slot(n, offset):
    return OFFSETS[n].index(n // 2 if offset == -(n // 2) else offset)


class RingGather:
    def __init__(self, n, neighbour, far, own, view, send, recv):
        self.n, self.neighbour, self.far, self.own = n, neighbour, far, own
        self.view, self.send, self.recv = view, send, recv

    def reach(self, direction):
        return self.n // 2 if direction == self.far else self.n // 2 - 1

    def copy(self, direction, step):
        d = 0 if direction == self.far else 1
        src = self.own if step == 1 else self.view(slot(self.n, -direction * (step - 1)))
        return remote(
            src,
            self.view(slot(self.n, -direction * step)),
            self.send.at[d, step - 1],
            self.recv.at[d, step - 1],
            self.neighbour(direction),
        )

    def start(self):
        for direction in (self.far, -self.far):
            self.copy(direction, 1).start()

    def stage(self, step, arrived=None):
        for direction in (self.far, -self.far):
            if step <= self.reach(direction):
                self.copy(direction, step).wait_recv()
                if step < self.reach(direction):
                    self.copy(direction, step + 1).start()
                if arrived is not None:
                    arrived(slot(self.n, -direction * step))

    def finish(self):
        for direction in (self.far, -self.far):
            for step in range(1, self.reach(direction) + 1):
                self.copy(direction, step).wait_send()


class Parcel:
    def __init__(self, out, out_scale, into, into_scale, send, recv, device):
        self.out, self.out_scale = out, out_scale
        self.into, self.into_scale = into, into_scale
        self.data = remote(out, into, send.at[0], recv.at[0], device)
        self.scale = remote(out_scale, into_scale, send.at[1], recv.at[1], device)

    def go(self):
        self.scale.start()
        self.data.start()

    def start(self, value):
        top = jnp.max(jnp.abs(value), axis=0, keepdims=True)
        top = jnp.maximum(jnp.max(top, axis=1, keepdims=True), 1e-30)
        self.out_scale[...] = jnp.broadcast_to(top * (1 / 32767.0), (8, 128))
        self.scale.start()
        self.out[...] = (
            jnp.round(value * (32767.0 / top)).astype(jnp.int32).astype(jnp.int16)
        )
        self.data.start()

    def arrive(self):
        self.data.wait_recv()
        self.scale.wait_recv()

    def take(self):
        self.arrive()
        return self.into[...].astype(jnp.int32).astype(jnp.float32) * self.into_scale[0:1, 0:1]

    def sent(self):
        self.data.wait_send()
        self.scale.wait_send()


class RingReduce:
    def __init__(self, n, neighbour, far, part, box):
        self.n, self.neighbour, self.far, self.part, self.box = n, neighbour, far, part, box

    def steps(self, direction):
        return self.n // 2 if direction == self.far else self.n // 2 - 1

    def parcel(self, direction, step):
        out, out_scale, into, into_scale, send, recv = self.box
        i = step - 1 if direction == self.far else self.n // 2 + step - 1
        return Parcel(
            out.at[i], out_scale.at[i], into.at[i], into_scale.at[i],
            send.at[i], recv.at[i], self.neighbour(direction),
        )

    def step(self, direction, step):
        if step > self.steps(direction):
            return
        value = self.part(slot(self.n, direction * (self.steps(direction) + 1 - step)))
        if step > 1:
            value = value + self.parcel(direction, step - 1).take()
        self.parcel(direction, step).start(value)

    def both(self, step):
        self.step(self.far, step)
        self.step(-self.far, step)

    def last(self):
        value = self.part(slot(self.n, 0))
        for direction in (self.far, -self.far):
            value = value + self.parcel(direction, self.steps(direction)).take()
        return value

    def finish(self):
        for direction in (self.far, -self.far):
            for step in range(1, self.steps(direction) + 1):
                self.parcel(direction, step).sent()


def greet(at):
    barrier = pltpu.get_barrier_semaphore()
    others = [at.column(-1), at.column(1), at.diagonal(-1), at.diagonal(1), at.row(-1), at.row(1)]
    others += [at.line(-1), at.line(1), at.other_core(), at.twin(), at.twin(True)]
    for device in others:
        pl.semaphore_signal(barrier, inc=1, device_id=device, device_id_type=MESH)
    pl.semaphore_wait(barrier, len(others))


def coefficients(rows, cols, row_ids, col_ids, scale, bias):
    logits = lax.dot_general(
        rows, cols, (((1,), (1,)), ((), ())), preferred_element_type=jnp.float32
    )
    power = jnp.minimum(logits * (scale * -LOG2E) - bias * LOG2E, 126.0)
    sigmoid = 1.0 / (1.0 + jnp.exp2(power))
    label = jnp.where(row_ids == col_ids, 1.0, 0.0)
    return (sigmoid - label).astype(jnp.bfloat16)


def product(coef, rows):
    return jnp.dot(coef, rows, preferred_element_type=jnp.float32)


def product_t(coef, rows):
    return lax.dot_general(
        coef, rows, (((0,), (0,)), ((), ())), preferred_element_type=jnp.float32
    )


def kernel(
    scale, bias, ids_in, a_own, b_own, c_own, a_out, b_out, c_out, a_unit, b_unit, c_unit, all_ids, ids, ids_t,
    a, b, c, ga, gb, gc, coef_ab, coef_ca, coef_cb,
    a_near, a_box, a_box_scale, b_box, b_box_scale, c_box, c_box_scale, y_box, y_box_scale, sums,
    ga_send, ga_recv, gb_send, gb_recv, gc_send, gc_recv, gt_send, gt_recv, gx_send, gx_recv, own_sem,
    ra_send, ra_recv, rb_send, rb_recv, rc_send, rc_recv, ry_send, ry_recv, rt_send, rt_recv, re_send, re_recv,
):
    at = Place()

    def span(start, size):
        return pl.ds(pl.multiple_of(start, 16), size)

    k = (at.c + at.xh) % 2
    my_b, my_c, my_a = span(at.c * HALF, HALF), span(k * HALF, HALF), span(at.xh * HALF, HALF)
    my_quarter = span(at.xh * HALF + at.c * QUARTER, QUARTER)

    def a_quarter(i, core):
        return a.at[span(i * HALF + core * QUARTER, QUARTER)]

    def piece(ref, i):
        return ref.at[i * HALF : (i + 1) * HALF]

    def quarter(ref, i, part):
        return ref.at[span(i * HALF + part * QUARTER, QUARTER)]

    def c_gather(q):
        own = c_own.at[span(k * HALF + q * QUARTER, QUARTER)]
        return RingGather(8, at.column, 1, own, lambda i: quarter(c, i, q), gc_send.at[q], gc_recv.at[q])

    def b_gather(q):
        return RingGather(4, at.row, 1 - 2 * q, b_share(q), lambda i: quarter(b, i, q), gb_send.at[q], gb_recv.at[q])

    def b_share(q):
        return b_own.at[span(at.c * HALF + q * QUARTER, QUARTER)]

    ring_c = [c_gather(q) for q in range(2)]
    ring_b = [b_gather(q) for q in range(2)]
    ring_a = RingGather(8, at.diagonal, -1, a_own.at[my_quarter], lambda i: a_quarter(i, at.c), ga_send, ga_recv)
    own = [
        pltpu.make_async_copy(a_own.at[my_a], piece(a, 7), own_sem.at[0]),
        pltpu.make_async_copy(b_own.at[my_b], piece(b, 3), own_sem.at[1]),
        pltpu.make_async_copy(c_own.at[my_c], piece(c, 7), own_sem.at[2]),
    ]

    def pass_over(i, core):
        view = a_quarter(i, core)
        return remote(view, view, gt_send.at[i], gt_recv.at[i], at.other_core())

    def over_x(i, q):
        src = b_share(q) if i == 3 else quarter(b, i, q)
        return remote(src, quarter(b, 4 + i, q), gx_send.at[q, i], gx_recv.at[q, i], at.line(1 - 2 * q))

    done = set()

    def once(key, wait):
        if key not in done:
            done.add(key)
            wait()

    def to_other(i):
        pass_over(i, at.c).start()

    def gather_a(step):
        ring_a.stage(step, to_other)

    def gather_b(step):
        for q in range(2):
            ring_b[q].stage(step, lambda i: over_x(i, q).start())

    def b_start():
        for q in range(2):
            ring_b[q].start()

    def x_start():
        for q in range(2):
            over_x(3, q).start()

    def a_here(*groups):
        once("own", lambda: [copy.wait() for copy in own])
        for i in (i for g in groups or range(4) for i in (2 * g, 2 * g + 1)):
            if i < 7:
                once(("a", i), lambda: pass_over(i, 1 - at.c).wait_recv())

    def b_here():
        once("own", lambda: [copy.wait() for copy in own])
        for i in range(4):
            for q in range(2):
                once(("b", i, q), lambda: over_x(i, q).wait_recv())

    def c_here(g):
        once("own", lambda: [copy.wait() for copy in own])

    def ab_rows(g):
        a_here(g)
        b_here()
        rows = pl.ds(g * ROWS, ROWS)
        tile = coefficients(a[rows, :], b[...], ids_t[rows, 0:1], ids[1:2, 0:BLOCK], scale[0], bias[0])
        coef_ab[rows, :] = tile
        ga[rows, :] = scale[0] * product(tile, b[...])

    def cb_rows(g):
        b_here()
        c_here(g)
        rows = pl.ds(g * ROWS, ROWS)
        tile = coefficients(c[rows, :], b[...], ids_t[rows, 2:3], ids[1:2, 0:BLOCK], scale[2], bias[2])
        coef_cb[rows, :] = tile
        gc[rows, :] = scale[2] * product(tile, b[...])

    def ca_rows(g):
        a_here()
        c_here(g)
        rows = pl.ds(g * ROWS, ROWS)
        tile = coefficients(c[rows, :], a[...], ids_t[rows, 2:3], ids[0:1, 0:BLOCK], scale[1], bias[1])
        coef_ca[rows, :] = tile
        gc[rows, :] = gc[rows, :] + scale[1] * product(tile, a[...])

    def a_cols(i):
        cols = pl.ds(i * TILE, TILE)
        ga[cols, :] = ga[cols, :] + scale[1] * product_t(coef_ca[:, cols], c[...])

    def b_cols(i):
        cols = pl.ds(i * TILE, TILE)
        gb[cols, :] = scale[0] * product_t(coef_ab[:, cols], a[...]) + scale[2] * product_t(coef_cb[:, cols], c[...])

    def a_part(i):
        once(("near", i), lambda: near(i, 1 - at.c).wait_recv())
        return ga[pl.ds(pl.multiple_of(i * HALF + at.c * QUARTER, 8), QUARTER), :] + a_near[i]

    reduce_a = RingReduce(
        8, at.diagonal, -1, a_part,
        (a_box.at[0], a_box_scale.at[0], a_box.at[1], a_box_scale.at[1], ra_send, ra_recv),
    )

    def c_ring(q):
        def part(i):
            return gc[i * HALF + q * QUARTER : i * HALF + (q + 1) * QUARTER, :]

        return RingReduce(
            8, at.column, 1, part,
            (c_box.at[0, q], c_box_scale.at[0, q], c_box.at[1, q], c_box_scale.at[1, q], rc_send.at[q], rc_recv.at[q]),
        )

    reduce_c = [c_ring(q) for q in range(2)]
    def x_ring(h):
        next_part = (at.xh + at.xl) % 2
        places = ((0, 1 - at.xh), (1, next_part), (1, 1 - next_part), (0, at.xh))

        def part(i):
            r, quarter_of = places[i]
            return jnp.concatenate(
                [gb[pl.ds(pl.multiple_of((4 * r + 2 * h + j) * HALF + quarter_of * QUARTER, 8), QUARTER), :] for j in range(2)]
            )

        return RingReduce(
            4, at.line, 1 - 2 * h, part,
            (b_box.at[0, h], b_box_scale.at[0, h], b_box.at[1, h], b_box_scale.at[1, h], rb_send.at[h], rb_recv.at[h]),
        )

    reduce_x = [x_ring(h) for h in range(2)]
    reduce_y = RingReduce(
        4, at.row, 1, lambda i: sums[i // 2, i % 2 * QUARTER : (i % 2 + 1) * QUARTER, :],
        (y_box.at[0], y_box_scale.at[0], y_box.at[1], y_box_scale.at[1], ry_send, ry_recv),
    )

    def near(i, core):
        return remote(
            ga.at[pl.ds(pl.multiple_of(i * HALF + core * QUARTER, 8), QUARTER)], a_near.at[i],
            rt_send.at[i], rt_recv.at[i], at.other_core(),
        )

    def rows_of(half, part):
        return span(half * HALF + part * QUARTER, QUARTER)

    def ready(out, unit, half, part, i, device):
        rows, number = out.at[rows_of(half, part)], unit.at[2 * half + part]
        return Parcel(rows, number, rows, number, re_send.at[i], re_recv.at[i], device)

    def to_twin(i):
        if i < 2:
            return ready(c_out.at[at.xh], c_unit.at[at.xh], k, i, i, at.twin(True))
        if i == 2:
            return ready(b_out, b_unit, at.c, at.xh, i, at.twin())
        return ready(a_out, a_unit, at.xh, at.c, i, at.twin())

    def from_twin(i):
        if i < 2:
            return ready(c_out.at[1 - at.xh], c_unit.at[1 - at.xh], k, i, i, at.twin(True))
        if i == 2:
            return ready(b_out, b_unit, at.c, 1 - at.xh, i, at.twin())
        return ready(a_out, a_unit, 1 - at.xh, at.c, i, at.twin())

    def to_core(i, other):
        chip = 1 - at.xh if other else at.xh
        j = 4 + 2 * i + other
        if i < 2:
            return ready(c_out.at[chip], c_unit.at[chip], k, i, j, at.other_core())
        if i == 2:
            return ready(b_out, b_unit, at.c, chip, j, at.other_core())
        return ready(a_out, a_unit, chip, at.c, j, at.other_core())

    def from_core(i, other):
        chip = 1 - at.xh if other else at.xh
        j = 4 + 2 * i + other
        if i < 2:
            return ready(c_out.at[chip], c_unit.at[chip], 1 - k, i, j, at.other_core())
        if i == 2:
            return ready(b_out, b_unit, 1 - at.c, chip, j, at.other_core())
        return ready(a_out, a_unit, chip, 1 - at.c, j, at.other_core())

    def mine_done(i, value):
        to_twin(i).start(value)
        to_core(i, 0).go()

    def other_done(i):
        from_twin(i).arrive()
        to_core(i, 1).go()

    def near_go(i):
        for j in ((0, 1), (2, 3, 4), (5, 6, 7))[i]:
            near(j, 1 - at.c).start()

    def b_last(r):
        sums[r] = reduce_x[r].last()

    steps = {
        "sA": ring_a.start,
        "sC": ring_c[0].start,
        "sD": ring_c[1].start,
        "sP": b_start,
        "sX": x_start,
        "P1": lambda: gather_b(1),
        "P2": lambda: gather_b(2),
        "La": lambda: mine_done(3, reduce_a.last()),
        "Ly": lambda: mine_done(2, reduce_y.last()),
        "Oa": lambda: other_done(3),
        "Ob": lambda: other_done(2),
    }
    for i in range(1, 5):
        steps[f"A{i}"] = lambda i=i: gather_a(i)
        steps[f"C{i}"] = lambda i=i: ring_c[0].stage(i)
        steps[f"D{i}"] = lambda i=i: ring_c[1].stage(i)
    for i in range(4):
        steps[f"ab{i}"] = lambda i=i: ab_rows(i)
        steps[f"cb{i}"] = lambda i=i: cb_rows(i)
        steps[f"ca{i}"] = lambda i=i: ca_rows(i)
    for i in range(3):
        steps[f"ac{i}"] = lambda i=i: a_cols(i)
        steps[f"bc{i}"] = lambda i=i: b_cols(i)
        steps[f"ns{i}"] = lambda i=i: near_go(i)
    for q in range(2):
        steps[f"Lx{q}"] = lambda q=q: b_last(q)
        steps[f"Lc{q}"] = lambda q=q: mine_done(q, reduce_c[q].last())
        steps[f"Sc{q}"] = lambda q=q: other_done(q)
    for name, ring in (("a", reduce_a), ("x0", reduce_x[0]), ("x1", reduce_x[1]), ("c0", reduce_c[0]), ("c1", reduce_c[1]), ("y", reduce_y)):
        for way, direction in (("f", ring.far), ("n", -ring.far)):
            for i in range(1, ring.steps(direction) + 1):
                steps[f"{name}{way}{i}"] = lambda ring=ring, d=direction, i=i: ring.step(d, i)

    def shards_of(which):
        if which == 0:
            return [at.diagonal(o)[0] for o in OFFSETS[8]], at.xh
        if which == 1:
            return [at.at(xl=xl, y=(at.y + o + 4) % 4)[0] for xl in (at.xl, 1 - at.xl) for o in OFFSETS[4]], at.c
        return [at.column(o)[0] for o in OFFSETS[8]], k

    def lay_out_ids():
        ids_copy.wait()
        ids[...] = jnp.zeros_like(ids)
        lane = lax.broadcasted_iota(jnp.int32, (3, 256), 1)
        row = lax.broadcasted_iota(jnp.int32, (3, 256), 0)
        for which in range(3):
            shards, half = shards_of(which)
            for i, shard in enumerate(shards):
                base = shard * ROWS + half * HALF
                start = base // 128 * 128 - base // (TOKENS - HALF) * 128
                window = all_ids[:, pl.ds(pl.multiple_of(start, 128), 256)]
                first = i * HALF % 128
                moved = pltpu.roll(window, (first - base + start + 256) % 256, 1)
                here = (row == which) & (lane >= first) & (lane < first + HALF)
                place = (slice(0, 3), slice(i * HALF - first, i * HALF - first + 256))
                ids[place] = jnp.where(here, moved, ids[place])
        ids_t[...] = jnp.transpose(ids[:, 0:BLOCK])

    ids_copy = pltpu.make_async_copy(ids_in, all_ids, own_sem.at[3])
    steps["ids"] = lay_out_ids
    ids_copy.start()
    for copy in own:
        copy.start()
    greet(at)
    for name in ORDER:
        steps[name]()

    for ring in (ring_a, *ring_c, *ring_b, reduce_a, reduce_y, *reduce_c, *reduce_x):
        ring.finish()
    for i in range(7):
        pass_over(i, at.c).wait_send()
    for i in range(4):
        for q in range(2):
            over_x(i, q).wait_send()
    for i in range(8):
        near(i, 1 - at.c).wait_send()
    for i in range(4):
        to_twin(i).sent()
        for other in range(2):
            to_core(i, other).sent()
            from_core(i, other).arrive()


def gradients(scale, bias, ids, a, b, c):
    vmem = pl.BlockSpec(memory_space=pltpu.VMEM)
    smem = pl.BlockSpec(memory_space=pltpu.SMEM)
    hbm = pl.BlockSpec(memory_space=pl.ANY)
    dma = pltpu.SemaphoreType.DMA
    f32, bf16, i16 = jnp.float32, jnp.bfloat16, jnp.int16
    m = pltpu.VMEM
    shape = jax.ShapeDtypeStruct
    a, b, c, a_unit, b_unit, c_unit = pl.pallas_call(
        kernel,
        out_shape=(
            shape((ROWS, WIDTH), i16), shape((ROWS, WIDTH), i16), shape((2, ROWS, WIDTH), i16),
            shape((4, 8, 128), f32), shape((4, 8, 128), f32), shape((2, 4, 8, 128), f32),
        ),
        in_specs=[smem, smem] + [hbm] * 4,
        out_specs=(vmem,) * 6,
        scratch_shapes=[
            m((3, TOKENS), jnp.int32), m((8, 896), jnp.int32), m((BLOCK, 8), jnp.int32),
            m((BLOCK, WIDTH), bf16), m((BLOCK, WIDTH), bf16), m((BLOCK, WIDTH), bf16),
            m((BLOCK, WIDTH), f32), m((BLOCK, WIDTH), f32), m((BLOCK, WIDTH), f32),
            m((BLOCK, BLOCK), bf16), m((BLOCK, BLOCK), bf16), m((BLOCK, BLOCK), bf16),
            m((8, QUARTER, WIDTH), f32),
            m((2, 7, QUARTER, WIDTH), i16), m((2, 7, 8, 128), f32),
            m((2, 2, 3, HALF, WIDTH), i16), m((2, 2, 3, 8, 128), f32),
            m((2, 2, 7, QUARTER, WIDTH), i16), m((2, 2, 7, 8, 128), f32),
            m((2, 3, QUARTER, WIDTH), i16), m((2, 3, 8, 128), f32),
            m((2, HALF, WIDTH), f32),
            dma((2, 4)), dma((2, 4)), dma((2, 2, 2)), dma((2, 2, 2)), dma((2, 2, 4)), dma((2, 2, 4)),
            dma((7,)), dma((7,)), dma((2, 4)), dma((2, 4)), dma((4,)),
            dma((7, 2)), dma((7, 2)), dma((2, 3, 2)), dma((2, 3, 2)), dma((2, 7, 2)), dma((2, 7, 2)), dma((3, 2)), dma((3, 2)),
            dma((8,)), dma((8,)), dma((12, 2)), dma((12, 2)),
        ],
        compiler_params=pltpu.CompilerParams(
            collective_id=0, has_side_effects=True, vmem_limit_bytes=56 << 20
        ),
    )(scale, bias, ids, a, b, c)
    return decode(a, b, c, a_unit, b_unit, c_unit)


def decode_kernel(
    a, b, c, a_unit, b_unit, c_unit, a_out, b_out, c_out, codes, units, values, sems
):
    jobs = ((a, a_unit, 0), (b, b_unit, 1), (c.at[0], c_unit.at[0], 2), (c.at[1], c_unit.at[1], 3))
    reads = [
        (
            pltpu.make_async_copy(code, codes.at[i], sems.at[0, i]),
            pltpu.make_async_copy(unit, units.at[i], sems.at[1, i]),
        )
        for code, unit, i in jobs
    ]
    for pair in reads:
        for copy in pair:
            copy.start()

    def value(i, j):
        code = codes[i, j * QUARTER : (j + 1) * QUARTER, :]
        return code.astype(jnp.int32).astype(jnp.float32) * units[i, j, 0:1, 0:1]

    writes = []
    for n, (terms, out) in enumerate((((0,), a_out), ((1,), b_out), ((2, 3), c_out))):
        for i in terms:
            for copy in reads[i]:
                copy.wait()
        for j in range(4):
            total = value(terms[0], j)
            if len(terms) == 2:
                total = total + value(terms[1], j)
            values[n, j * QUARTER : (j + 1) * QUARTER, :] = total
        writes.append(pltpu.make_async_copy(values.at[n], out, sems.at[2, n]))
        writes[-1].start()
    for copy in writes:
        copy.wait()


def decode(a, b, c, a_unit, b_unit, c_unit):
    hbm = pl.BlockSpec(memory_space=pl.ANY)
    out = jax.ShapeDtypeStruct((ROWS, WIDTH), jnp.float32)
    return pl.pallas_call(
        decode_kernel,
        out_shape=(out, out, out),
        in_specs=[hbm] * 6,
        out_specs=(hbm, hbm, hbm),
        scratch_shapes=[
            pltpu.VMEM((4, ROWS, WIDTH), jnp.int16),
            pltpu.VMEM((4, 4, 8, 128), jnp.float32),
            pltpu.VMEM((3, ROWS, WIDTH), jnp.float32),
            pltpu.SemaphoreType.DMA((3, 4)),
        ],
        compiler_params=pltpu.CompilerParams(vmem_limit_bytes=56 << 20),
    )(a, b, c, a_unit, b_unit, c_unit)


def body(event, lidar, frame, sample_ids, logit_scale, logit_bias):
    return gradients(logit_scale, logit_bias, sample_ids, event, lidar, frame)


def solution(mesh):
    placed = (P("dp", None), P("dp", None), P("dp", None), P(), P(), P())
    return jax.shard_map(
        body,
        mesh=mesh,
        in_specs=placed,
        out_specs=(P("dp", None), P("dp", None), P("dp", None)),
        check_vma=False,
    )
```
